32 devices in a mesh: dp: 16 (over z, y, x), mp: 2 (over core).
Axes of the slice: x: 2, y: 2, z: 4, core: 2. Of those that a mesh axis runs over, the one named last changes fastest.
Arguments:
- tokens: bfloat16 [16384, 768], P('dp'), may hold values from -6 to 6
- cotangent: bfloat16 [16384, 768], P('dp'), may hold values from -6 to 6
- lengths: int32 [16, 24], P('dp'), may hold values from 1 to 200, 1024 in all within a row
- query_weight: bfloat16 [768, 768], P(None, 'mp'), may hold values from -0.21875 to 0.21875
- query_bias: float32 [768], P('mp'), may hold values from -3 to 3
- key_weight: bfloat16 [768, 768], P(None, 'mp'), may hold values from -0.21875 to 0.21875
- value_weight: bfloat16 [768, 768], P(None, 'mp'), may hold values from -0.21875 to 0.21875
- value_bias: float32 [768], P('mp'), may hold values from -3 to 3
- output_weight: bfloat16 [768, 768], P('mp'), may hold values from -1.25 to 1.25
- output_bias: float32 [768], replicated, may hold values from -3 to 3
- first_gain: float32 [768], replicated, may hold values from 0.5 to 1.5
- first_shift: float32 [768], replicated, may hold values from -3 to 3
- up_weight: bfloat16 [768, 3072], P(None, 'mp'), may hold values from -0.21875 to 0.21875
- up_bias: float32 [3072], P('mp'), may hold values from -3 to 3
- down_weight: bfloat16 [3072, 768], P('mp'), may hold values from -0.21875 to 0.21875
- down_bias: float32 [768], replicated, may hold values from -3 to 3
- second_gain: float32 [768], replicated, may hold values from 0.5 to 1.5
- second_shift: float32 [768], replicated, may hold values from -3 to 3
Outputs:
- layer_output: bfloat16 [16384, 768], P('dp')
- tokens_grad: bfloat16 [16384, 768], P('dp')
- query_weight_grad: float32 [768, 768], P(None, 'mp')
- query_bias_grad: float32 [768], P('mp')
- key_weight_grad: float32 [768, 768], P(None, 'mp')
- value_weight_grad: float32 [768, 768], P(None, 'mp')
- value_bias_grad: float32 [768], P('mp')
- output_weight_grad: float32 [768, 768], P('mp')
- output_bias_grad: float32 [768], replicated
- first_gain_grad: float32 [768], replicated
- first_shift_grad: float32 [768], replicated
- up_weight_grad: float32 [768, 3072], P(None, 'mp')
- up_bias_grad: float32 [3072], P('mp')
- down_weight_grad: float32 [3072, 768], P('mp')
- down_bias_grad: float32 [768], replicated
- second_gain_grad: float32 [768], replicated
- second_shift_grad: float32 [768], replicated
The draws below stay inside these ranges and needn't reach their ends.
Inputs may be any that keep to these rules, and one draw needn't show every extreme that they name: Each row holds the lengths of the 23 sequences packed on one index of dp, in order, then the length of its padding run; each row sums to 1024 and its largest entry is 200.
All inputs are finite; a program needn't handle non-finite values.
Results may differ from the reference program's by a relative error of at most 0.024.
Values may be sent and summed in bfloat16 or wider, within the bound.
A program may use at most 192 MiB of HBM per device.

```python
import math
import jax
import jax.numpy as jnp
import numpy as np
from jax import lax

D = 768
HEADS = 12
HEAD_DIM = 64
FF = 3072
TOK_DEV = 1024
SEQS = 24
SEQ_MOST = 200
GROUPS = 16
TOKENS = 16384
N_MP = 2


def level_of(rng, dims, pieces, smallest, top_value):
    factor_of, own = 1.0, jax.random.fold_in(rng, 6)
    for dim, blocks in pieces:
        heights = jnp.exp(jax.random.uniform(jax.random.fold_in(own, dim), (blocks,), jnp.float32, smallest / len(pieces), top_value / len(pieces)))
        factor_of = factor_of * jnp.repeat(heights, dims[dim] // blocks).reshape([-1 if axis == dim else 1 for axis in range(len(dims))])
    return factor_of


def split_up(amount, total, bound, skew):
    loads = [(1 << 20) // math.isqrt(grade ** skew) + 1 for grade in range(2, amount + 1)]
    spare, given = total - bound - (amount - 1), [1] * (amount - 1)
    while spare > 0:
        movable = [i for i in range(amount - 1) if given[i] < bound]
        whole, remaining = sum([loads[i] for i in movable]), spare
        for i in movable:
            extra = min(bound - given[i], max(1, remaining * loads[i] // whole), spare)
            given[i] = given[i] + extra
            spare = spare - extra
    return np.array([bound] + given)


def ragged_sizes(stream_key, number_of, total, bound, lean):
    if number_of == 2:
        one = jax.random.randint(stream_key, (), max(1, total - bound), min(bound, total - 1) + 1)
        return jnp.stack([one, total - one])
    sizes = jnp.asarray(split_up(number_of, total, bound, lean), jnp.int32)
    pairs = (number_of - 1) // 2
    source_of, sink = sizes[1:1 + 2 * pairs:2], sizes[2:2 + 2 * pairs:2]
    room = jnp.minimum(source_of - 1, bound - sink)
    moved = jax.random.randint(jax.random.fold_in(stream_key, 1), (pairs,), 0, 1 << 20) % (room + 1)
    sizes = sizes.at[1:1 + 2 * pairs:2].set(source_of - moved).at[2:2 + 2 * pairs:2].set(sink + moved)
    return sizes[jax.random.permutation(jax.random.fold_in(stream_key, 2), number_of)]


def bell_draw(stream_key, extent, scale, limit, pieces=(), kind=jnp.bfloat16):
    drawn = scale * jax.random.normal(stream_key, extent, jnp.float32)
    if pieces:
        drawn = drawn * level_of(stream_key, extent, pieces, -0.22, 0.18)
    return jnp.clip(drawn, -limit, limit).astype(kind)


def setup_inputs(seed: int = 0) -> dict:
    keys = jax.random.split(jax.random.key(seed), 19)
    return {
        "tokens": bell_draw(keys[0], (TOKENS, D), 1.0, 6.0, ((0, 16),)),
        "cotangent": bell_draw(keys[1], (TOKENS, D), 1.0, 6.0, ((0, 16),)),
        "lengths": jax.vmap(lambda own: ragged_sizes(own, SEQS, TOK_DEV, SEQ_MOST, 2))(jax.random.split(keys[2], GROUPS)).reshape((GROUPS, SEQS)).astype(jnp.int32),
        "query_weight": bell_draw(keys[3], (D, D), D ** -0.5, 0.21875, ((1, 2),)),
        "query_bias": bell_draw(keys[4], (D,), 0.5, 3.0, ((0, 2),), jnp.float32),
        "key_weight": bell_draw(keys[5], (D, D), D ** -0.5, 0.21875, ((1, 2),)),
        "value_weight": bell_draw(keys[6], (D, D), D ** -0.5, 0.21875, ((1, 2),)),
        "value_bias": bell_draw(keys[7], (D,), 0.5, 3.0, ((0, 2),), jnp.float32),
        "output_weight": bell_draw(keys[8], (D, D), (D // 32) ** -0.5, 1.25, ((0, 2),)),
        "output_bias": bell_draw(keys[9], (D,), 0.5, 3.0, (), jnp.float32),
        "first_gain": jnp.clip(1.0 + 0.1 * jax.random.normal(keys[10], (D,), jnp.float32), 0.5, 1.5),
        "first_shift": bell_draw(keys[11], (D,), 0.5, 3.0, (), jnp.float32),
        "up_weight": bell_draw(keys[12], (D, FF), D ** -0.5, 0.21875, ((1, 2),)),
        "up_bias": bell_draw(keys[13], (FF,), 0.5, 3.0, ((0, 2),), jnp.float32),
        "down_weight": bell_draw(keys[14], (FF, D), (FF // 4) ** -0.5, 0.21875, ((0, 2),)),
        "down_bias": bell_draw(keys[15], (D,), 0.5, 3.0, (), jnp.float32),
        "second_gain": jnp.clip(1.0 + 0.1 * jax.random.normal(keys[16], (D,), jnp.float32), 0.5, 1.5),
        "second_shift": bell_draw(keys[17], (D,), 0.5, 3.0, (), jnp.float32),
    }


EPSILON = 1e-12
NEGATIVE = -1e+30
HIGHEST = lax.Precision.HIGHEST

@jax.custom_vjp
def low(v):
    return lax.optimization_barrier(v.astype(jnp.bfloat16)).astype(jnp.float32)

@jax.custom_vjp
def low_back(v):
    return v

def low_keep(v):
    return (low(v), None)

def low_pass(kept, grad):
    return (grad,)

def back_keep(v):
    return (v, None)

def back_low(kept, grad):
    return (low(grad),)
low.defvjp(low_keep, low_pass)
low_back.defvjp(back_keep, back_low)

def rounded(value):
    return low(low_back(value))

def layer_norm(hidden, norm_gain, norm_shift):
    row_mean = lax.optimization_barrier(jnp.mean(hidden, axis=-1, keepdims=True))
    centered = hidden - row_mean
    variance = lax.optimization_barrier(jnp.mean(centered * centered, axis=-1, keepdims=True))
    return centered * lax.rsqrt(variance + EPSILON) * norm_gain + norm_shift

def group_forward(params, group_tokens, segment):
    query_weight, query_bias, key_weight, value_weight, value_bias, output_weight, output_bias, first_gain, first_shift, up_weight, up_bias, down_weight, down_bias, second_gain, second_shift = params
    row_count = group_tokens.shape[0]
    shard_width = D // N_MP
    shard_hidden = FF // N_MP
    heads_shard = HEADS // N_MP
    score_scale = 1.0 / math.sqrt(HEAD_DIM)
    same_segment = segment[:, None] == segment[None, :]
    tokens_low = low(group_tokens)
    attention = jnp.zeros((row_count, D), jnp.float32)
    for shard in range(N_MP):
        col_range = slice(shard * shard_width, (shard + 1) * shard_width)
        shard_tokens = low_back(tokens_low)
        query = rounded(jnp.dot(shard_tokens, query_weight[:, col_range], precision=HIGHEST) + query_bias[col_range])
        key_part = rounded(jnp.dot(shard_tokens, key_weight[:, col_range], precision=HIGHEST))
        value_part = rounded(jnp.dot(shard_tokens, value_weight[:, col_range], precision=HIGHEST) + value_bias[col_range])
        query_heads = query.reshape(row_count, heads_shard, HEAD_DIM)
        key_heads = key_part.reshape(row_count, heads_shard, HEAD_DIM)
        value_heads = value_part.reshape(row_count, heads_shard, HEAD_DIM)
        raw_scores = jnp.einsum('qhd,khd->hqk', query_heads, key_heads, precision=HIGHEST) * score_scale
        scores = jnp.where(same_segment[None], low_back(raw_scores), NEGATIVE)
        probabilities = low(jax.nn.softmax(scores, axis=-1))
        context = jnp.einsum('hqk,khd->qhd', probabilities, value_heads, precision=HIGHEST)
        context = rounded(context.reshape(row_count, shard_width))
        attention = attention + low(jnp.dot(context, output_weight[col_range, :], precision=HIGHEST))
    hidden = group_tokens + low_back(attention) + output_bias
    first = layer_norm(hidden, first_gain, first_shift)
    first_low = low(first)
    feed = jnp.zeros((row_count, D), jnp.float32)
    for shard in range(N_MP):
        hid_range = slice(shard * shard_hidden, (shard + 1) * shard_hidden)
        shard_first = low_back(first_low)
        pre_act = low_back(jnp.dot(shard_first, up_weight[:, hid_range], precision=HIGHEST) + up_bias[hid_range])
        inner = low(jax.nn.gelu(pre_act, approximate=False))
        feed = feed + low(jnp.dot(inner, down_weight[hid_range, :], precision=HIGHEST))
    return layer_norm(first + low_back(feed) + down_bias, second_gain, second_shift)

def reference(tokens, cotangent, lengths, query_weight, query_bias, key_weight, value_weight, value_bias, output_weight, output_bias, first_gain, first_shift, up_weight, up_bias, down_weight, down_bias, second_gain, second_shift):
    group_count = lengths.shape[0]
    seq_ends = jnp.cumsum(lengths, axis=1)
    places = jnp.arange(TOK_DEV, dtype=jnp.int32)
    segments = lax.optimization_barrier(jnp.sum((places[None, :, None] >= seq_ends[:, None, :]).astype(jnp.int32), axis=2))
    live_rows = (segments < SEQS - 1).astype(jnp.float32)
    group_tokens = tokens.astype(jnp.float32).reshape(group_count, TOK_DEV, D)
    params = tuple((item.astype(jnp.float32) for item in (query_weight, query_bias, key_weight, value_weight, value_bias, output_weight, output_bias, first_gain, first_shift, up_weight, up_bias, down_weight, down_bias, second_gain, second_shift)))

    def forward(weights, inputs):

        def one_group(carried):
            return group_forward(weights, carried[0], carried[1])
        return lax.map(jax.checkpoint(one_group), (inputs, segments))
    result, pullback = jax.vjp(forward, params, group_tokens)
    seed_grad = cotangent.astype(jnp.float32).reshape(group_count, TOK_DEV, D) * live_rows[:, :, None]
    weight_grads, token_grads = pullback(seed_grad)
    grad_qw, grad_qb, grad_kw, grad_vw, grad_vb, grad_ow, grad_ob, grad_ga, grad_sa, grad_uw, grad_ub, grad_dw, grad_db, grad_gb, grad_sb = weight_grads
    return (result.reshape(group_count * TOK_DEV, D).astype(jnp.bfloat16), token_grads.reshape(group_count * TOK_DEV, D).astype(jnp.bfloat16), grad_qw, grad_qb, grad_kw, grad_vw, grad_vb, grad_ow, grad_ob, grad_ga, grad_sa, grad_uw, grad_ub, grad_dw, grad_db, grad_gb, grad_sb)
```

```python
import functools
import math

import jax
import jax.numpy as jnp
from jax import lax
from jax.experimental import pallas as pl
from jax.experimental.pallas import tpu as pltpu
from jax.sharding import PartitionSpec as P

HEAD_DIM = 64
MESH = pl.DeviceIdType.MESH


EPSILON = 1e-12
NEGATIVE = -1e30
ROW_TILE = 16


def bits_of(count):
    bits, stride = [], 1
    while stride < count:
        bits.append(stride)
        stride *= 2
    return bits


def exchange_orders(count):
    bits = bits_of(count)
    if len(bits) < 3:
        return [bits, bits[::-1]]
    return [[bits[0], bits[2], bits[1]] + bits[3:], [bits[1], bits[2], bits[0]] + bits[3:]]


def plan_steps(rows, order):
    halvings, wholes, length = [], [], rows
    for stride in order:
        if (length // 2) % ROW_TILE == 0 and length % 2 == 0:
            length //= 2
            halvings.append((stride, length, "halve"))
        else:
            wholes.append((stride, length, "whole"))
    gathers = [(stride, sent, "gather") for stride, sent, _ in reversed(halvings)]
    return halvings + wholes + gathers


def landing_rows(steps):
    return sum(sent for _, sent, kind in steps if kind != "gather")


class Reduction:
    def __init__(self, block, total, landing, send_sem, recv_sem, steps, rows, dp, mp):
        self.total, self.landing, self.send_sem, self.recv_sem = total, landing, send_sem, recv_sem
        self.steps, self.dp, self.mp = steps, dp, mp
        self.held, self.base = block, 0
        self.low, self.offset = 0, 0
        self.copies, self.next_step = [], 0

    def side(self, stride):
        return (self.dp // stride) % 2

    def advance(self):
        step = self.next_step
        if step > 0:
            self.finish(step - 1)
        if step < len(self.steps):
            self.start(step)
        self.next_step += 1

    def start(self, step):
        stride, sent, kind = self.steps[step]
        side = self.side(stride)
        if kind == "gather":
            rows = pl.ds(pl.multiple_of(self.low, ROW_TILE), sent)
            source, target = self.total.at[rows], self.total.at[rows]
        else:
            start = self.base + (1 - side) * sent if kind == "halve" else self.base
            source = self.held.at[pl.ds(pl.multiple_of(start, ROW_TILE), sent)]
            target = self.landing.at[pl.ds(self.offset, sent)]
        copy = pltpu.make_async_remote_copy(
            source,
            target,
            self.send_sem.at[step],
            self.recv_sem.at[step],
            device_id=(self.dp + stride - 2 * stride * side, self.mp),
            device_id_type=MESH,
        )
        copy.start()
        self.copies.append(copy)

    def finish(self, step):
        stride, sent, kind = self.steps[step]
        side = self.side(stride)
        self.copies[step].wait()
        if kind == "gather":
            self.low = self.low - side * sent
            return
        kept = self.base + side * sent if kind == "halve" else self.base
        if kind == "halve":
            self.low = self.low + side * sent
        last = step + 1 == len(self.steps) or (
            self.steps[step + 1][2] == "gather"
        )
        held, offset, low = self.held, self.offset, self.low
        part = sent
        while part > 64 and part % 2 == 0 and (part // 2) % ROW_TILE == 0:
            part //= 2

        def add(index, carry):
            own = pl.ds(pl.multiple_of(kept + index * part, ROW_TILE), part)
            came = pl.ds(pl.multiple_of(offset + index * part, ROW_TILE), part)
            both = held[own].astype(jnp.float32) + self.landing[came].astype(jnp.float32)
            if last:
                done = pl.ds(pl.multiple_of(low + index * part, ROW_TILE), part)
                self.total[done] = both.astype(self.total.dtype)
            else:
                self.landing[came] = both.astype(self.landing.dtype)
            return carry

        lax.fori_loop(0, sent // part, add, 0)
        self.held, self.base = self.landing, offset
        self.offset += sent


def reduce_kernel(plans, schedule, strides, *refs):
    count = len(plans)
    parts, sums, landings = refs[:count], refs[count : 2 * count], refs[2 * count : 3 * count]
    send_sems, recv_sems = refs[3 * count : 4 * count], refs[4 * count : 5 * count]
    dp, mp = lax.axis_index("dp"), lax.axis_index("mp")
    barrier = pltpu.get_barrier_semaphore()
    for stride in strides:
        partner = dp + stride - 2 * stride * ((dp // stride) % 2)
        pl.semaphore_signal(barrier, inc=1, device_id=(partner, mp), device_id_type=MESH)
    pl.semaphore_wait(barrier, len(strides))
    chains = [
        Reduction(parts[c], sums[c], landings[c], send_sems[c], recv_sems[c], plans[c], parts[c].shape[0], dp, mp)
        for c in range(count)
    ]
    for c in schedule:
        chains[c].advance()


def sum_over_dp(blocks, vectors, dp_size):
    if dp_size == 1:
        return blocks, vectors
    orders = exchange_orders(dp_size)
    arrays = list(blocks) + [vectors]
    plans = [plan_steps(b.shape[0], orders[i % 2]) for i, b in enumerate(blocks)]
    plans.append([(stride, vectors.shape[0], "whole") for stride in orders[0]])
    begin = [i // 2 for i in range(len(blocks))] + [0]
    schedule = []
    for turn in range(max(begin) + max(len(p) for p in plans) + 1):
        for c, plan in enumerate(plans):
            if 0 <= turn - begin[c] <= len(plan):
                schedule.append(c)
    vmem = pl.BlockSpec(memory_space=pltpu.VMEM)
    landing = [
        pltpu.VMEM((landing_rows(plan), a.shape[1]), a.dtype) for plan, a in zip(plans, arrays)
    ]
    sems = [pltpu.SemaphoreType.DMA((len(plan),)) for plan in plans]
    sums = pl.pallas_call(
        functools.partial(reduce_kernel, plans, schedule, bits_of(dp_size)),
        out_shape=[jax.ShapeDtypeStruct(a.shape, a.dtype) for a in arrays],
        in_specs=[vmem] * len(arrays),
        out_specs=[vmem] * len(arrays),
        scratch_shapes=landing + sems + sems,
        compiler_params=pltpu.CompilerParams(
            collective_id=0, has_side_effects=True, vmem_limit_bytes=48 * 2**20
        ),
        name="sum_over_dp",
    )(*arrays)
    return sums[:-1], sums[-1]


def layer_norm(hidden, norm_gain, norm_shift):
    row_mean = jnp.mean(hidden, axis=-1, keepdims=True)
    centered = hidden - row_mean
    variance = jnp.mean(centered * centered, axis=-1, keepdims=True)
    return centered * lax.rsqrt(variance + EPSILON) * norm_gain + norm_shift


def gelu_exact(pre_act):
    return jax.nn.gelu(pre_act, approximate=False)


def contract_rows(left, right):
    return lax.dot_general(
        left, right, (((0,), (0,)), ((), ())), preferred_element_type=jnp.float32
    )


def times_transposed(left, right):
    return lax.dot_general(
        left, right, (((1,), (1,)), ((), ())), preferred_element_type=jnp.float32
    )


def masked_scores(query_heads, key_heads, same_segment, score_scale):
    raw_scores = (
        jnp.einsum("qhd,khd->hqk", query_heads, key_heads, preferred_element_type=jnp.float32)
        * score_scale
    )
    return jnp.where(same_segment[None], raw_scores, NEGATIVE)


def local(
    tokens,
    cotangent,
    lengths,
    query_weight,
    query_bias,
    key_weight,
    value_weight,
    value_bias,
    output_weight,
    output_bias,
    first_gain,
    first_shift,
    up_weight,
    up_bias,
    down_weight,
    down_bias,
    second_gain,
    second_shift,
):
    row_count = tokens.shape[0]
    shard_width = query_weight.shape[1]
    heads_shard = shard_width // HEAD_DIM
    score_scale = 1.0 / math.sqrt(HEAD_DIM)
    seq_ends = jnp.cumsum(lengths[0])
    places = jnp.arange(row_count, dtype=jnp.int32)
    segment = jnp.sum((places[:, None] >= seq_ends[None, :]).astype(jnp.int32), axis=1)
    same_segment = segment[:, None] == segment[None, :]
    live_rows = (segment < lengths.shape[1] - 1).astype(jnp.float32)
    tokens_wide = tokens.astype(jnp.float32)
    query = (jnp.dot(tokens, query_weight, preferred_element_type=jnp.float32) + query_bias).astype(
        jnp.bfloat16
    )
    key_part = jnp.dot(tokens, key_weight, preferred_element_type=jnp.float32).astype(jnp.bfloat16)
    value_part = (
        jnp.dot(tokens, value_weight, preferred_element_type=jnp.float32) + value_bias
    ).astype(jnp.bfloat16)
    query_heads = query.reshape(row_count, heads_shard, HEAD_DIM)
    key_heads = key_part.reshape(row_count, heads_shard, HEAD_DIM)
    value_heads = value_part.reshape(row_count, heads_shard, HEAD_DIM)
    scores = masked_scores(query_heads, key_heads, same_segment, score_scale)
    log_total = jax.nn.logsumexp(scores, axis=-1, keepdims=True)
    probabilities = jnp.exp(scores - log_total)
    context = jnp.einsum(
        "hqk,khd->qhd",
        probabilities.astype(jnp.bfloat16),
        value_heads,
        preferred_element_type=jnp.float32,
    )
    context = context.reshape(row_count, shard_width).astype(jnp.bfloat16)
    attention = lax.psum(
        jnp.dot(context, output_weight, preferred_element_type=jnp.float32).astype(jnp.bfloat16),
        "mp",
    ).astype(jnp.float32)
    hidden = tokens_wide + attention + output_bias
    first, first_pull = jax.vjp(layer_norm, hidden, first_gain, first_shift)
    first_low = first.astype(jnp.bfloat16)
    inner, gelu_pull = jax.vjp(
        gelu_exact, jnp.dot(first_low, up_weight, preferred_element_type=jnp.float32) + up_bias
    )
    inner_low = inner.astype(jnp.bfloat16)
    feed = lax.psum(
        jnp.dot(inner_low, down_weight, preferred_element_type=jnp.float32).astype(jnp.bfloat16),
        "mp",
    ).astype(jnp.float32)
    result, second_pull = jax.vjp(layer_norm, first + feed + down_bias, second_gain, second_shift)
    grad_out = cotangent.astype(jnp.float32) * live_rows[:, None]
    d_resid, second_gain_grad, second_shift_grad = second_pull(grad_out)
    down_bias_grad = jnp.sum(d_resid, axis=0)
    feed_grad = d_resid.astype(jnp.bfloat16)
    down_weight_grad = contract_rows(inner_low, feed_grad)
    d_inner = times_transposed(feed_grad, down_weight)
    d_pre = gelu_pull(d_inner)[0].astype(jnp.bfloat16)
    up_weight_grad = contract_rows(first_low, d_pre)
    up_bias_grad = jnp.sum(d_pre.astype(jnp.float32), axis=0)
    d_first = d_resid + lax.psum(
        times_transposed(d_pre, up_weight).astype(jnp.bfloat16), "mp"
    ).astype(jnp.float32)
    d_hidden, first_gain_grad, first_shift_grad = first_pull(d_first)
    output_bias_grad = jnp.sum(d_hidden, axis=0)
    hidden_grad = d_hidden.astype(jnp.bfloat16)
    output_weight_grad = contract_rows(context, hidden_grad)
    d_context = times_transposed(hidden_grad, output_weight).astype(jnp.bfloat16)
    d_context = d_context.reshape(row_count, heads_shard, HEAD_DIM)
    probabilities = jnp.exp(
        masked_scores(query_heads, key_heads, same_segment, score_scale) - log_total
    )
    d_values = jnp.einsum(
        "hqk,qhd->khd",
        probabilities.astype(jnp.bfloat16),
        d_context,
        preferred_element_type=jnp.float32,
    ).astype(jnp.bfloat16)
    d_probs = jnp.einsum("qhd,khd->hqk", d_context, value_heads, preferred_element_type=jnp.float32)
    d_scores = probabilities * (d_probs - jnp.sum(d_probs * probabilities, axis=-1, keepdims=True))
    d_scores = d_scores.astype(jnp.bfloat16)
    d_query = (
        (
            jnp.einsum("hqk,khd->qhd", d_scores, key_heads, preferred_element_type=jnp.float32)
            * score_scale
        )
        .astype(jnp.bfloat16)
        .reshape(row_count, shard_width)
    )
    d_keys = (
        (
            jnp.einsum("hqk,qhd->khd", d_scores, query_heads, preferred_element_type=jnp.float32)
            * score_scale
        )
        .astype(jnp.bfloat16)
        .reshape(row_count, shard_width)
    )
    d_values = d_values.reshape(row_count, shard_width)
    query_weight_grad = contract_rows(tokens, d_query)
    key_weight_grad = contract_rows(tokens, d_keys)
    value_weight_grad = contract_rows(tokens, d_values)
    query_bias_grad = jnp.sum(d_query.astype(jnp.float32), axis=0)
    value_bias_grad = jnp.sum(d_values.astype(jnp.float32), axis=0)
    token_part = (
        times_transposed(d_query, query_weight)
        + times_transposed(d_keys, key_weight)
        + times_transposed(d_values, value_weight)
    )
    tokens_grad = (
        d_hidden + lax.psum(token_part.astype(jnp.bfloat16), "mp").astype(jnp.float32)
    ).astype(jnp.bfloat16)
    half = shard_width
    low = lambda grad: grad.astype(jnp.bfloat16)
    attention_side = [
        jnp.concatenate([low(query_weight_grad), low(key_weight_grad)], axis=1),
        jnp.concatenate(
            [
                low(value_weight_grad),
                jnp.concatenate(
                    [low(output_weight_grad[:, :half]), low(output_weight_grad[:, half:])], axis=0
                ),
            ],
            axis=1,
        ),
    ]
    width = tokens.shape[1]
    up_low, down_low = low(up_weight_grad), low(down_weight_grad)
    blocks = [
        down_low[:width],
        down_low[width:],
        up_low[:, :width],
        up_low[:, width:],
        *attention_side,
    ]
    vectors = [
        query_bias_grad,
        value_bias_grad,
        output_bias_grad,
        first_gain_grad,
        first_shift_grad,
        up_bias_grad,
        down_bias_grad,
        second_gain_grad,
        second_shift_grad,
    ]
    sizes = [v.shape[0] for v in vectors]
    flat = jnp.concatenate(vectors)
    rows = -(-flat.shape[0] // (128 * ROW_TILE)) * ROW_TILE
    flat = jnp.pad(flat, (0, rows * 128 - flat.shape[0])).reshape(rows, 128)
    blocks, flat = sum_over_dp(blocks, flat, lax.axis_size("dp"))
    flat = flat.reshape(-1)
    starts = [sum(sizes[:i]) for i in range(len(sizes))]
    (
        query_bias_grad,
        value_bias_grad,
        output_bias_grad,
        first_gain_grad,
        first_shift_grad,
        up_bias_grad,
        down_bias_grad,
        second_gain_grad,
        second_shift_grad,
    ) = [flat[a : a + n] for a, n in zip(starts, sizes)]
    wide = lambda total: total.astype(jnp.float32)
    down_weight_grad = jnp.concatenate([wide(blocks[0]), wide(blocks[1])], axis=0)
    up_weight_grad = jnp.concatenate([wide(blocks[2]), wide(blocks[3])], axis=1)
    query_weight_grad, key_weight_grad = wide(blocks[4][:, :half]), wide(blocks[4][:, half:])
    value_weight_grad = wide(blocks[5][:, :half])
    output_weight_grad = jnp.concatenate(
        [wide(blocks[5][:half, half:]), wide(blocks[5][half:, half:])], axis=1
    )
    return (
        result.astype(jnp.bfloat16),
        tokens_grad,
        query_weight_grad,
        query_bias_grad,
        key_weight_grad,
        value_weight_grad,
        value_bias_grad,
        output_weight_grad,
        output_bias_grad,
        first_gain_grad,
        first_shift_grad,
        up_weight_grad,
        up_bias_grad,
        down_weight_grad,
        down_bias_grad,
        second_gain_grad,
        second_shift_grad,
    )


def solution(mesh):
    in_specs = (
        P("dp", None),
        P("dp", None),
        P("dp", None),
        P(None, "mp"),
        P("mp"),
        P(None, "mp"),
        P(None, "mp"),
        P("mp"),
        P("mp", None),
        P(),
        P(),
        P(),
        P(None, "mp"),
        P("mp"),
        P("mp", None),
        P(),
        P(),
        P(),
    )
    out_specs = (
        P("dp", None),
        P("dp", None),
        P(None, "mp"),
        P("mp"),
        P(None, "mp"),
        P(None, "mp"),
        P("mp"),
        P("mp", None),
        P(),
        P(),
        P(),
        P(None, "mp"),
        P("mp"),
        P("mp", None),
        P(),
        P(),
        P(),
    )
    return jax.shard_map(local, mesh=mesh, in_specs=in_specs, out_specs=out_specs, check_vma=False)
```

```python
import functools
import math

import jax
import jax.numpy as jnp
from jax import lax
from jax.experimental import pallas as pl
from jax.experimental.pallas import tpu as pltpu
from jax.sharding import PartitionSpec as P

HEAD_DIM = 64
PAIR = 2 * HEAD_DIM
LONGEST = 200
BLOCK = 256
STRIP = 32
MESH = pl.DeviceIdType.MESH


EPSILON = 1e-12
NEGATIVE = -1e30
ROW_TILE = 16


def bits_of(count):
    bits, stride = [], 1
    while stride < count:
        bits.append(stride)
        stride *= 2
    return bits


def exchange_orders(count):
    bits = bits_of(count)
    if len(bits) < 3:
        return [bits, bits[::-1]]
    return [[bits[0], bits[2], bits[1]] + bits[3:], [bits[1], bits[2], bits[0]] + bits[3:]]


def plan_steps(rows, order):
    halvings, wholes, length = [], [], rows
    for stride in order:
        if (length // 2) % ROW_TILE == 0 and length % 2 == 0:
            length //= 2
            halvings.append((stride, length, "halve"))
        else:
            wholes.append((stride, length, "whole"))
    gathers = [(stride, sent, "gather") for stride, sent, _ in reversed(halvings)]
    return halvings + wholes + gathers


def landing_rows(steps):
    return sum(sent for _, sent, kind in steps if kind != "gather")


class Reduction:
    def __init__(self, block, total, landing, send_sem, recv_sem, steps, dp, mp):
        self.total, self.landing, self.send_sem, self.recv_sem = total, landing, send_sem, recv_sem
        self.steps, self.dp, self.mp = steps, dp, mp
        self.held, self.base = block, 0
        self.low, self.offset = 0, 0
        self.copies, self.next_step = [], 0

    def side(self, stride):
        return (self.dp // stride) % 2

    def advance(self):
        step = self.next_step
        if step > 0:
            self.finish(step - 1)
        if step < len(self.steps):
            self.start(step)
        self.next_step += 1

    def start(self, step):
        stride, sent, kind = self.steps[step]
        side = self.side(stride)
        if kind == "gather":
            rows = pl.ds(pl.multiple_of(self.low, ROW_TILE), sent)
            source, target = self.total.at[rows], self.total.at[rows]
        else:
            start = self.base + (1 - side) * sent if kind == "halve" else self.base
            source = self.held.at[pl.ds(pl.multiple_of(start, ROW_TILE), sent)]
            target = self.landing.at[pl.ds(self.offset, sent)]
        copy = pltpu.make_async_remote_copy(
            source,
            target,
            self.send_sem.at[step],
            self.recv_sem.at[step],
            device_id=(self.dp + stride - 2 * stride * side, self.mp),
            device_id_type=MESH,
        )
        copy.start()
        self.copies.append(copy)

    def finish(self, step):
        stride, sent, kind = self.steps[step]
        side = self.side(stride)
        self.copies[step].wait()
        if kind == "gather":
            self.low = self.low - side * sent
            return
        kept = self.base + side * sent if kind == "halve" else self.base
        if kind == "halve":
            self.low = self.low + side * sent
        last = step + 1 == len(self.steps) or (
            self.steps[step + 1][2] == "gather"
        )
        held, offset, low = self.held, self.offset, self.low
        part = sent
        while part > 64 and part % 2 == 0 and (part // 2) % ROW_TILE == 0:
            part //= 2

        def add(index, carry):
            own = pl.ds(pl.multiple_of(kept + index * part, ROW_TILE), part)
            came = pl.ds(pl.multiple_of(offset + index * part, ROW_TILE), part)
            both = held[own].astype(jnp.float32) + self.landing[came].astype(jnp.float32)
            if last:
                done = pl.ds(pl.multiple_of(low + index * part, ROW_TILE), part)
                self.total[done] = both.astype(self.total.dtype)
            else:
                self.landing[came] = both.astype(self.landing.dtype)
            return carry

        lax.fori_loop(0, sent // part, add, 0)
        self.held, self.base = self.landing, offset
        self.offset += sent


def dot(left, right, left_dim, right_dim):
    return lax.dot_general(
        left, right, (((left_dim,), (right_dim,)), ((), ())), preferred_element_type=jnp.float32
    )


def column_sums(values):
    return jnp.sum(values.reshape(values.shape[0] // 8, 8, values.shape[1]), axis=0)


def key_window(block, row_count):
    low = max(0, (block * BLOCK - (LONGEST - 1)) // 128 * 128)
    high = min(row_count, -(-((block + 1) * BLOCK + LONGEST - 1) // 128) * 128)
    return low, high


def layer_kernel(
    plans,
    vector_plan,
    strides,
    tokens_hbm,
    cotangent_hbm,
    lengths,
    query_weight_hbm,
    key_weight_hbm,
    value_weight_hbm,
    output_weight_hbm,
    up_weight_hbm,
    down_weight_hbm,
    query_bias,
    value_bias,
    output_bias,
    first_gain,
    first_shift,
    up_bias,
    down_bias,
    second_gain,
    second_shift,
    result_hbm,
    tokens_grad_hbm,
    *refs,
):
    count = len(plans)
    totals, vector_total = refs[:count], refs[count]
    (
        tokens,
        cotangent,
        qkv_weight,
        output_weight,
        up_weight,
        down_weight,
        qkv,
        context,
        log_totals,
        segment_row,
        segment_column,
        parts,
        landed,
        first_hat,
        first_scale,
        first_low,
        slope,
        inner,
        d_pre,
        d_resid,
        grad_low,
        down_blocks,
        up_blocks,
        vector_sums,
        up_bias_sums,
        vectors,
        block_landings,
        vector_landing,
        load_sem,
        store_sem,
        part_send,
        part_recv,
        chain_send,
        chain_recv,
        vector_send,
        vector_recv,
    ) = refs[count + 1 :]
    row_count, width = tokens.shape
    shard = context.shape[1]
    hidden = inner.shape[1]
    blocks = row_count // BLOCK
    strips = BLOCK // STRIP
    pairs = shard // PAIR
    dp, mp = lax.axis_index("dp"), lax.axis_index("mp")
    other = 1 - mp

    barrier = pltpu.get_barrier_semaphore()
    for stride in strides:
        partner = dp + stride - 2 * stride * ((dp // stride) % 2)
        pl.semaphore_signal(barrier, inc=1, device_id=(partner, mp), device_id_type=MESH)
    pl.semaphore_signal(barrier, inc=1, device_id=(dp, other), device_id_type=MESH)

    loads = [
        pltpu.make_async_copy(source, target, load_sem.at[i])
        for i, (source, target) in enumerate(
            [
                (tokens_hbm, tokens),
                (query_weight_hbm, qkv_weight.at[:, :shard]),
                (key_weight_hbm, qkv_weight.at[:, shard : 2 * shard]),
                (value_weight_hbm, qkv_weight.at[:, 2 * shard :]),
                (output_weight_hbm, output_weight),
                (up_weight_hbm, up_weight),
                (down_weight_hbm, down_weight),
                (cotangent_hbm, cotangent),
            ]
        )
    ]
    for copy in loads:
        copy.start()

    runs = lengths.shape[1]
    row_place = lax.broadcasted_iota(jnp.int32, (1, row_count), 1)
    column_place = lax.broadcasted_iota(jnp.int32, (row_count, 1), 0)
    in_row, in_column = jnp.zeros_like(row_place), jnp.zeros_like(column_place)
    end = 0
    for run in range(runs):
        end = end + lengths[0, run]
        in_row = in_row + (row_place >= end).astype(jnp.int32)
        in_column = in_column + (column_place >= end).astype(jnp.int32)
    segment_row[...] = in_row
    segment_column[...] = in_column
    vector_sums[...] = jnp.zeros_like(vector_sums)
    up_bias_sums[...] = jnp.zeros_like(up_bias_sums)
    vectors[...] = jnp.zeros_like(vectors)

    head_lanes = lax.broadcasted_iota(jnp.int32, (1, PAIR), 1) < HEAD_DIM
    keep_head = [
        head_lanes.astype(jnp.float32).astype(jnp.bfloat16),
        (1.0 - head_lanes.astype(jnp.float32)).astype(jnp.bfloat16),
    ]

    def rows_of(block):
        return pl.ds(pl.multiple_of(block * BLOCK, BLOCK), BLOCK)

    def strip_of(block, strip):
        return pl.ds(pl.multiple_of(block * BLOCK + strip * STRIP, STRIP), STRIP)

    def part_copy(turn, block):
        rows = rows_of(block)
        return pltpu.make_async_remote_copy(
            parts.at[turn % 2, rows],
            landed.at[turn % 2, rows],
            part_send.at[turn, block],
            part_recv.at[turn, block],
            device_id=(dp, other),
            device_id_type=MESH,
        )

    def both_parts(turn, rows):
        return parts[turn % 2, rows, :].astype(jnp.float32) + landed[turn % 2, rows, :].astype(
            jnp.float32
        )

    def send_part(turn, block, value):
        if turn >= 2:
            part_copy(turn - 2, block).wait_send()
        parts[turn % 2, rows_of(block), :] = value.astype(jnp.bfloat16)
        part_copy(turn, block).start()

    def each(number, body, unroll=1):
        lax.fori_loop(0, number, lambda i, carry: (body(i), carry)[1], 0, unroll=unroll)

    def add_vector(place, values):
        vector_sums[place] = vector_sums[place] + column_sums(values)

    for copy in loads[:4]:
        copy.wait()
    scale = 1.0 / math.sqrt(HEAD_DIM)

    def project(block):
        rows = rows_of(block)
        got = dot(tokens[rows, :], qkv_weight[...], 1, 0)
        qkv[rows, :shard] = ((got[:, :shard] + query_bias[...]) * scale).astype(jnp.bfloat16)
        qkv[rows, shard : 2 * shard] = got[:, shard : 2 * shard].astype(jnp.bfloat16)
        qkv[rows, 2 * shard :] = (got[:, 2 * shard :] + value_bias[...]).astype(jnp.bfloat16)

    for block in range(blocks):
        project(block)

    def pair_inputs(block, pair):
        low, high = key_window(block, row_count)
        rows = pl.ds(block * BLOCK, BLOCK)
        keys = pl.ds(low, high - low)
        at = lambda group: pl.ds(pl.multiple_of(group * shard + pair * PAIR, PAIR), PAIR)
        bias = jnp.where(segment_column[keys, :] == segment_row[:, rows], 0.0, NEGATIVE)
        return rows, keys, qkv[rows, at(0)], qkv[keys, at(1)], qkv[keys, at(2)], bias, at

    def attend(block, pair):
        rows, keys, query, key, value, bias, at = pair_inputs(block, pair)
        outs = []
        for head in range(2):
            scores = dot(key, query * keep_head[head], 1, 1) + bias
            top = jnp.max(scores, axis=0, keepdims=True)
            raised = jnp.exp(scores - top)
            total = jnp.sum(raised, axis=0, keepdims=True)
            log_totals[2 * pair + head, :, rows] = top + jnp.log(total)
            weights = (raised * (1.0 / total)).astype(jnp.bfloat16)
            outs.append(dot(weights, value, 0, 0))
        context[rows, at(0)] = jnp.where(head_lanes, outs[0], outs[1]).astype(jnp.bfloat16)

    for copy in loads[4:]:
        copy.wait()
    for block in range(blocks):
        each(pairs, functools.partial(attend, block))
        if block == 0:
            pl.semaphore_wait(barrier, len(strides) + 1)
        send_part(0, block, dot(context[rows_of(block), :], output_weight[...], 1, 0))

    def normalized(values):
        centered = values - jnp.mean(values, axis=-1, keepdims=True)
        variance = jnp.mean(centered * centered, axis=-1, keepdims=True)
        inverse = lax.rsqrt(variance + EPSILON)
        return centered * inverse, inverse

    def pull_norm(grad, hat, inverse):
        return inverse * (
            grad
            - jnp.mean(grad, axis=-1, keepdims=True)
            - hat * jnp.mean(grad * hat, axis=-1, keepdims=True)
        )

    def feed_forward(block):
        part_copy(0, block).wait_recv()

        def norm(strip):
            rows = strip_of(block, strip)
            hat, inverse = normalized(
                tokens[rows, :].astype(jnp.float32) + both_parts(0, rows) + output_bias[...]
            )
            first_hat[rows, :] = hat
            first_scale[rows, :] = inverse
            first_low[rows, :] = (hat * first_gain[...] + first_shift[...]).astype(jnp.bfloat16)

        each(strips, norm, 2)
        rows = rows_of(block)
        tile = hidden // 4
        for start in range(0, hidden, tile):
            some = slice(start, start + tile)
            pre = dot(first_low[rows, :], up_weight[:, some], 1, 0) + up_bias[:, some]
            below = 0.5 + 0.5 * lax.erf(pre * math.sqrt(0.5))
            density = jnp.exp(-0.5 * pre * pre) * (1.0 / math.sqrt(2.0 * math.pi))
            inner[rows, some] = (pre * below).astype(jnp.bfloat16)
            slope[rows, some] = (below + pre * density).astype(jnp.bfloat16)
        send_part(1, block, dot(inner[rows, :], down_weight[...], 1, 0))

    each(blocks, feed_forward)

    def second_norm(block):
        part_copy(1, block).wait_recv()

        def norm(strip):
            rows = strip_of(block, strip)
            first = first_hat[rows, :] * first_gain[...] + first_shift[...]
            hat, inverse = normalized(first + both_parts(1, rows) + down_bias[...])
            live = (segment_column[rows, :] < runs - 1).astype(jnp.float32)
            grad = cotangent[rows, :].astype(jnp.float32) * live
            cotangent[rows, :] = (hat * second_gain[...] + second_shift[...]).astype(jnp.bfloat16)
            back = pull_norm(grad * second_gain[...], hat, inverse)
            d_resid[rows, :] = back
            grad_low[rows, :] = back.astype(jnp.bfloat16)
            add_vector(4, grad * hat)
            add_vector(5, grad)
            add_vector(3, back)

        each(strips, norm, 2)

    each(blocks, second_norm)
    result_store = pltpu.make_async_copy(cotangent, result_hbm, store_sem.at[0])
    result_store.start()

    at_attention = lambda place: inner.at[:width, place * width : (place + 1) * width]
    sources = [down_blocks.at[0], down_blocks.at[1], up_blocks.at[0], up_blocks.at[1]]
    sources += [at_attention(0), at_attention(1)]
    chains = [
        Reduction(
            sources[c],
            totals[c],
            block_landings.at[c],
            chain_send.at[c],
            chain_recv.at[c],
            plans[c],
            dp,
            mp,
        )
        for c in range(count)
    ]
    vector_chain = Reduction(
        vectors, vector_total, vector_landing, vector_send, vector_recv, vector_plan, dp, mp
    )

    def advance(*which):
        for c in which:
            (vector_chain if c == count else chains[c]).advance()

    half = width // 2
    for place in range(2):
        for start in range(0, width, half):
            some = slice(place * width + start, place * width + start + half)
            down_blocks[place, start : start + half, :] = dot(
                inner[:, some], grad_low[...], 0, 0
            ).astype(jnp.bfloat16)
        advance(place)

    def through_hidden(block):
        rows = rows_of(block)
        tile = hidden // 4
        for start in range(0, hidden, tile):
            some = slice(start, start + tile)
            grad = dot(grad_low[rows, :], down_weight[some, :], 1, 1)
            low = (grad * slope[rows, some].astype(jnp.float32)).astype(jnp.bfloat16)
            d_pre[rows, some] = low
            up_bias_sums[:, some] = up_bias_sums[:, some] + column_sums(low.astype(jnp.float32))
        send_part(2, block, dot(d_pre[rows, :], up_weight[...], 1, 1))

    each(blocks, through_hidden)

    for place in range(2):
        some = slice(place * width, (place + 1) * width)
        for start in range(0, width, half):
            up_blocks[place, start : start + half, :] = dot(
                first_low[:, start : start + half], d_pre[:, some], 0, 0
            ).astype(jnp.bfloat16)
        advance(2 + place)

    def first_norm_back(block):
        part_copy(2, block).wait_recv()

        def norm(strip):
            rows = strip_of(block, strip)
            grad = d_resid[rows, :] + both_parts(2, rows)
            hat = first_hat[rows, :]
            back = pull_norm(grad * first_gain[...], hat, first_scale[rows, :])
            d_resid[rows, :] = back
            grad_low[rows, :] = back.astype(jnp.bfloat16)
            add_vector(1, grad * hat)
            add_vector(2, grad)
            add_vector(0, back)

        each(strips, norm, 2)
        rows = rows_of(block)
        d_pre[rows, :shard] = dot(grad_low[rows, :], output_weight[...], 1, 1).astype(jnp.bfloat16)

    each(blocks, first_norm_back)

    for start in range(0, width, shard):
        inner[start : start + shard, width + shard : 2 * width] = dot(
            context[...], grad_low[:, start : start + shard], 0, 0
        ).astype(jnp.bfloat16)

    first_hat[...] = jnp.zeros_like(first_hat)

    def attend_back(block, pair):
        rows, keys, query, key, value, bias, at = pair_inputs(block, pair)
        d_context = d_pre[rows, at(0)]
        d_key = d_value = 0.0
        d_query = []
        for head in range(2):
            own_query, own_grad = query * keep_head[head], d_context * keep_head[head]
            scores = dot(key, own_query, 1, 1) + bias
            weights = jnp.exp(scores - log_totals[2 * pair + head, :, rows])
            d_weights = dot(value, own_grad, 1, 1)
            mean = jnp.sum(weights * d_weights, axis=0, keepdims=True)
            d_scores = (weights * (d_weights - mean)).astype(jnp.bfloat16)
            d_value = d_value + dot(weights.astype(jnp.bfloat16), own_grad, 1, 0)
            d_key = d_key + dot(d_scores, own_query, 1, 0)
            d_query.append(dot(d_scores, key, 0, 0))
        slope[rows, at(0)] = (jnp.where(head_lanes, d_query[0], d_query[1]) * scale).astype(
            jnp.bfloat16
        )
        first_hat[keys, at(0)] = first_hat[keys, at(0)] + d_key
        first_hat[keys, at(1)] = first_hat[keys, at(1)] + d_value

    for block in range(blocks):
        each(pairs, functools.partial(attend_back, block))
        advance(*PUMP_ATTEND[block])

    def round_keys(strip):
        rows = pl.ds(pl.multiple_of(strip * STRIP, STRIP), STRIP)
        slope[rows, shard : 3 * shard] = first_hat[rows, :].astype(jnp.bfloat16)

    each(row_count // STRIP, round_keys, 4)

    for start in range(0, width, half):
        inner[start : start + half, :width] = dot(
            tokens[:, start : start + half], slope[:, :width], 0, 0
        ).astype(jnp.bfloat16)
    advance(4)
    inner[:width, width : width + shard] = dot(
        tokens[...], slope[:, width : width + shard], 0, 0
    ).astype(jnp.bfloat16)
    advance(5)

    def finish_vectors():
        for place in range(6):
            vectors[place : place + 1, :] = jnp.sum(vector_sums[place], axis=0, keepdims=True)
        up_sum = jnp.sum(up_bias_sums[...], axis=0, keepdims=True)
        for place in range(hidden // width):
            vectors[6 + place : 7 + place, :] = up_sum[:, place * width : (place + 1) * width]
        ones = jnp.ones((16, row_count), jnp.bfloat16)
        last = 6 + hidden // width
        vectors[last : last + 1, :shard] = dot(ones, slope[:, :shard], 1, 0)[:1]
        vectors[last : last + 1, shard:] = dot(ones, slope[:, 2 * shard : 3 * shard], 1, 0)[:1]

    finish_vectors()
    advance(count)

    def token_part(block):
        rows = rows_of(block)
        send_part(3, block, dot(slope[rows, : 3 * shard], qkv_weight[...], 1, 1))

    for block in range(blocks):
        token_part(block)
        advance(*PUMP_TOKENS[block])

    def tokens_back(block):
        part_copy(3, block).wait_recv()

        def total(strip):
            rows = strip_of(block, strip)
            tokens[rows, :] = (d_resid[rows, :] + both_parts(3, rows)).astype(jnp.bfloat16)

        each(strips, total, 2)

    each(blocks, tokens_back)
    tokens_store = pltpu.make_async_copy(tokens, tokens_grad_hbm, store_sem.at[1])
    tokens_store.start()

    left = chains + [vector_chain]
    for chain_order in TAIL_ORDER(left):
        chain_order.advance()

    for turn in (2, 3):
        for block in range(blocks):
            part_copy(turn, block).wait_send()
    result_store.wait()
    tokens_store.wait()


PUMP_ATTEND = [(0, 1), (), (0, 1, 2, 3), ()]
PUMP_TOKENS = [(), (), (), ()]


def TAIL_ORDER(chains):
    remaining = {i: len(c.steps) + 1 - c.next_step for i, c in enumerate(chains)}
    order = []
    while any(remaining.values()):
        for i, c in enumerate(chains):
            if remaining[i]:
                order.append(c)
                remaining[i] -= 1
    return order


def local(
    tokens,
    cotangent,
    lengths,
    query_weight,
    query_bias,
    key_weight,
    value_weight,
    value_bias,
    output_weight,
    output_bias,
    first_gain,
    first_shift,
    up_weight,
    up_bias,
    down_weight,
    down_bias,
    second_gain,
    second_shift,
):
    row_count, width = tokens.shape
    shard, hidden = query_weight.shape[1], up_weight.shape[1]
    dp_size = lax.axis_size("dp")
    blocks = row_count // BLOCK
    low, wide = jnp.bfloat16, jnp.float32
    count = 6
    orders = exchange_orders(dp_size)
    plans = [plan_steps(width, orders[i % 2]) for i in range(count)]
    vector_rows = ROW_TILE
    vector_plan = [(stride, vector_rows, "whole") for stride in orders[0]]
    landing = max(landing_rows(plan) for plan in plans)
    steps = max(len(plan) for plan in plans)
    hbm = pl.BlockSpec(memory_space=pl.ANY)
    vmem = pl.BlockSpec(memory_space=pltpu.VMEM)
    smem = pl.BlockSpec(memory_space=pltpu.SMEM)
    dma = pltpu.SemaphoreType.DMA
    flat = lambda v: v.reshape(1, -1)
    outs = pl.pallas_call(
        functools.partial(layer_kernel, plans, vector_plan, bits_of(dp_size)),
        out_shape=[
            jax.ShapeDtypeStruct((row_count, width), low),
            jax.ShapeDtypeStruct((row_count, width), low),
            *[jax.ShapeDtypeStruct((width, width), low)] * count,
            jax.ShapeDtypeStruct((vector_rows, width), wide),
        ],
        in_specs=[hbm, hbm, smem] + [hbm] * 6 + [vmem] * 9,
        out_specs=[hbm, hbm] + [vmem] * (count + 1),
        scratch_shapes=[
            pltpu.VMEM((row_count, width), low),
            pltpu.VMEM((row_count, width), low),
            pltpu.VMEM((width, 3 * shard), low),
            pltpu.VMEM((shard, width), low),
            pltpu.VMEM((width, hidden), low),
            pltpu.VMEM((hidden, width), low),
            pltpu.VMEM((row_count, 3 * shard), low),
            pltpu.VMEM((row_count, shard), low),
            pltpu.VMEM((shard // HEAD_DIM, 1, row_count), wide),
            pltpu.VMEM((1, row_count), jnp.int32),
            pltpu.VMEM((row_count, 1), jnp.int32),
            pltpu.VMEM((2, row_count, width), low),
            pltpu.VMEM((2, row_count, width), low),
            pltpu.VMEM((row_count, width), wide),
            pltpu.VMEM((row_count, 1), wide),
            pltpu.VMEM((row_count, width), low),
            pltpu.VMEM((row_count, hidden), low),
            pltpu.VMEM((row_count, hidden), low),
            pltpu.VMEM((row_count, hidden), low),
            pltpu.VMEM((row_count, width), wide),
            pltpu.VMEM((row_count, width), low),
            pltpu.VMEM((2, width, width), low),
            pltpu.VMEM((2, width, width), low),
            pltpu.VMEM((6, 8, width), wide),
            pltpu.VMEM((8, hidden), wide),
            pltpu.VMEM((vector_rows, width), wide),
            pltpu.VMEM((count, landing, width), low),
            pltpu.VMEM((max(1, len(vector_plan)) * vector_rows, width), wide),
            dma((8,)),
            dma((2,)),
            dma((4, blocks)),
            dma((4, blocks)),
            dma((count, steps)),
            dma((count, steps)),
            dma((max(1, len(vector_plan)),)),
            dma((max(1, len(vector_plan)),)),
        ],
        compiler_params=pltpu.CompilerParams(
            collective_id=0, has_side_effects=True, vmem_limit_bytes=63 * 2**20
        ),
        name="layer",
    )(
        tokens,
        cotangent,
        lengths,
        query_weight,
        key_weight,
        value_weight,
        output_weight,
        up_weight,
        down_weight,
        flat(query_bias),
        flat(value_bias),
        flat(output_bias),
        flat(first_gain),
        flat(first_shift),
        flat(up_bias),
        flat(down_bias),
        flat(second_gain),
        flat(second_shift),
    )
    result, tokens_grad, down_top, down_bottom, up_left, up_right, query_key, value_output, sums = (
        outs
    )
    f32 = lambda total: total.astype(jnp.float32)
    return (
        result,
        tokens_grad,
        f32(query_key[:, :shard]),
        sums[8, :shard],
        f32(query_key[:, shard:]),
        f32(value_output[:, :shard]),
        sums[8, shard:],
        f32(jnp.concatenate([value_output[:shard, shard:], value_output[shard:, shard:]], axis=1)),
        sums[0],
        sums[1],
        sums[2],
        f32(jnp.concatenate([up_left, up_right], axis=1)),
        sums[6:8].reshape(-1),
        f32(jnp.concatenate([down_top, down_bottom], axis=0)),
        sums[3],
        sums[4],
        sums[5],
    )


def solution(mesh):
    in_specs = (
        P("dp", None),
        P("dp", None),
        P("dp", None),
        P(None, "mp"),
        P("mp"),
        P(None, "mp"),
        P(None, "mp"),
        P("mp"),
        P("mp", None),
        P(),
        P(),
        P(),
        P(None, "mp"),
        P("mp"),
        P("mp", None),
        P(),
        P(),
        P(),
    )
    out_specs = (
        P("dp", None),
        P("dp", None),
        P(None, "mp"),
        P("mp"),
        P(None, "mp"),
        P(None, "mp"),
        P("mp"),
        P("mp", None),
        P(),
        P(),
        P(),
        P(None, "mp"),
        P("mp"),
        P("mp", None),
        P(),
        P(),
        P(),
    )
    return jax.shard_map(local, mesh=mesh, in_specs=in_specs, out_specs=out_specs, check_vma=False)
```

```python
import functools
import math

import jax
import jax.numpy as jnp
from jax import lax
from jax.experimental import pallas as pl
from jax.experimental.pallas import tpu as pltpu
from jax.sharding import PartitionSpec as P

HEAD_DIM = 64
PAIR = 2 * HEAD_DIM
LONGEST = 200
BLOCK = 256
STRIP = 32
MESH = pl.DeviceIdType.MESH


EPSILON = 1e-12
NEGATIVE = -1e30
ROW_TILE = 16


def bits_of(count):
    bits, stride = [], 1
    while stride < count:
        bits.append(stride)
        stride *= 2
    return bits


def exchange_orders(count):
    bits = bits_of(count)
    if len(bits) < 3:
        return [bits, bits[::-1]]
    a, b, c, *rest = bits
    return [[order[0], order[1], order[2], *rest] for order in ORDERS(a, b, c)]


def ORDERS(a, b, c):
    return [(a, b, c), (b, a, c)]


def plan_steps(rows, order):
    halvings, wholes, length = [], [], rows
    for stride in order:
        if (length // 2) % ROW_TILE == 0 and length % 2 == 0:
            length //= 2
            halvings.append((stride, length, "halve"))
        else:
            wholes.append((stride, length, "whole"))
    gathers = [(stride, sent, "gather") for stride, sent, _ in reversed(halvings)]
    return halvings + wholes + gathers


def landing_rows(steps):
    return sum(sent for _, sent, kind in steps if kind != "gather")


class Reduction:
    def __init__(self, block, total, landing, send_sem, recv_sem, steps, dp, mp, arrived):
        self.total, self.landing, self.send_sem, self.recv_sem = total, landing, send_sem, recv_sem
        self.steps, self.dp, self.mp, self.arrived = steps, dp, mp, arrived
        self.held, self.base = block, 0
        self.low, self.offset = 0, 0
        self.copies, self.next_step = [], 0

    def side(self, stride):
        return (self.dp // stride) % 2

    def advance(self):
        step = self.next_step
        if step > len(self.steps):
            return
        if step > 0:
            self.finish(step - 1)
        if step < len(self.steps):
            self.start(step)
        else:
            self.arrived()
        self.next_step += 1

    def start(self, step):
        stride, sent, kind = self.steps[step]
        side = self.side(stride)
        if kind == "gather":
            rows = pl.ds(pl.multiple_of(self.low, ROW_TILE), sent)
            source, target = self.total.at[rows], self.total.at[rows]
        else:
            start = self.base + (1 - side) * sent if kind == "halve" else self.base
            source = self.held.at[pl.ds(pl.multiple_of(start, ROW_TILE), sent)]
            target = self.landing.at[pl.ds(self.offset, sent)]
        copy = pltpu.make_async_remote_copy(
            source,
            target,
            self.send_sem.at[step],
            self.recv_sem.at[step],
            device_id=(self.dp + stride - 2 * stride * side, self.mp),
            device_id_type=MESH,
        )
        copy.start()
        self.copies.append(copy)

    def finish(self, step):
        stride, sent, kind = self.steps[step]
        side = self.side(stride)
        self.copies[step].wait()
        if kind == "gather":
            self.low = self.low - side * sent
            return
        kept = self.base + side * sent if kind == "halve" else self.base
        if kind == "halve":
            self.low = self.low + side * sent
        last = step + 1 == len(self.steps) or (
            self.steps[step + 1][2] == "gather"
        )
        held, offset, low = self.held, self.offset, self.low
        part = sent
        while part > 64 and part % 2 == 0 and (part // 2) % ROW_TILE == 0:
            part //= 2

        def add(index, carry):
            own = pl.ds(pl.multiple_of(kept + index * part, ROW_TILE), part)
            came = pl.ds(pl.multiple_of(offset + index * part, ROW_TILE), part)
            both = held[own].astype(jnp.float32) + self.landing[came].astype(jnp.float32)
            if last:
                done = pl.ds(pl.multiple_of(low + index * part, ROW_TILE), part)
                self.total[done] = both.astype(self.total.dtype)
            else:
                self.landing[came] = both.astype(self.landing.dtype)
            return carry

        lax.fori_loop(0, sent // part, add, 0)
        self.held, self.base = self.landing, offset
        self.offset += sent


def dot(left, right, left_dim, right_dim):
    return lax.dot_general(
        left, right, (((left_dim,), (right_dim,)), ((), ())), preferred_element_type=jnp.float32
    )


def column_sums(values):
    return jnp.sum(values.reshape(values.shape[0] // 8, 8, values.shape[1]), axis=0)


def key_window(block, row_count):
    low = max(0, (block * BLOCK - (LONGEST - 1)) // 128 * 128)
    high = min(row_count, -(-((block + 1) * BLOCK + LONGEST - 1) // 128) * 128)
    return low, high


def layer_kernel(
    plans,
    vector_plan,
    strides,
    tokens_hbm,
    cotangent_hbm,
    lengths,
    query_weight_hbm,
    key_weight_hbm,
    value_weight_hbm,
    output_weight_hbm,
    up_weight_hbm,
    down_weight_hbm,
    query_bias,
    value_bias,
    output_bias,
    first_gain,
    first_shift,
    up_bias,
    down_bias,
    second_gain,
    second_shift,
    result_hbm,
    tokens_grad_hbm,
    *refs,
):
    count = len(plans)
    sums_hbm, vector_total = refs[0], refs[1]
    (
        tokens,
        cotangent,
        qkv_weight,
        output_weight,
        up_weight,
        down_weight,
        qkv,
        context,
        log_totals,
        row_facts,
        run_of,
        not_run_of,
        parts,
        landed,
        first_hat,
        first_low,
        slope,
        inner,
        d_pre,
        d_resid,
        grad_low,
        down_blocks,
        up_blocks,
        vector_sums,
        up_bias_sums,
        vectors,
        block_landings,
        vector_landing,
        totals,
        bias_rows,
        load_sem,
        store_sem,
        part_send,
        part_recv,
        chain_send,
        chain_recv,
        vector_send,
        vector_recv,
        total_sem,
    ) = refs[2:]
    row_count, width = tokens.shape
    shard = context.shape[1]
    hidden = inner.shape[1]
    blocks = row_count // BLOCK
    strips = BLOCK // STRIP
    pairs = shard // PAIR
    dp, mp = lax.axis_index("dp"), lax.axis_index("mp")
    other = 1 - mp

    barrier = pltpu.get_barrier_semaphore()
    for stride in strides:
        partner = dp + stride - 2 * stride * ((dp // stride) % 2)
        pl.semaphore_signal(barrier, inc=1, device_id=(partner, mp), device_id_type=MESH)
    pl.semaphore_signal(barrier, inc=1, device_id=(dp, other), device_id_type=MESH)

    loads = [
        pltpu.make_async_copy(source, target, load_sem.at[i])
        for i, (source, target) in enumerate(
            [
                (tokens_hbm, tokens),
                (query_weight_hbm, qkv_weight.at[:, :shard]),
                (key_weight_hbm, qkv_weight.at[:, shard : 2 * shard]),
                (value_weight_hbm, qkv_weight.at[:, 2 * shard :]),
                (output_weight_hbm, output_weight),
                (up_weight_hbm, up_weight),
                (down_weight_hbm, down_weight),
                (cotangent_hbm, cotangent),
            ]
        )
    ]
    for copy in loads:
        copy.start()

    runs = lengths.shape[1]
    column_place = lax.broadcasted_iota(jnp.int32, (row_count, 1), 0)
    in_column = jnp.zeros_like(column_place)
    end = 0
    for run in range(runs):
        end = end + lengths[0, run]
        in_column = in_column + (column_place >= end).astype(jnp.int32)
    given = [query_bias, value_bias, output_bias, first_gain, first_shift, up_bias, down_bias]
    given += [second_gain, second_shift]
    for place, vector in enumerate(given):
        bias_rows[place : place + 1, : vector.shape[0]] = vector[...].reshape(1, -1)
    query_bias, value_bias = bias_rows.at[0:1, :shard], bias_rows.at[1:2, :shard]
    output_bias, first_gain, first_shift = [bias_rows.at[i : i + 1, :width] for i in (2, 3, 4)]
    up_bias = bias_rows.at[5:6, :]
    down_bias, second_gain, second_shift = [bias_rows.at[i : i + 1, :width] for i in (6, 7, 8)]
    row_facts[:, 0:1] = (in_column < runs - 1).astype(jnp.float32)
    vector_sums[...] = jnp.zeros_like(vector_sums)
    up_bias_sums[...] = jnp.zeros_like(up_bias_sums)
    vectors[...] = jnp.zeros_like(vectors)

    lane = lax.broadcasted_iota(jnp.int32, (1, PAIR), 1)
    head_lanes = lane < HEAD_DIM
    keep_head = [
        head_lanes.astype(jnp.float32).astype(jnp.bfloat16),
        (1.0 - head_lanes.astype(jnp.float32)).astype(jnp.bfloat16),
    ]
    spare = [lane - HEAD_DIM, jnp.where(head_lanes, lane, -1)]
    part_lanes = [[spare[head] == runs + part for part in range(3)] for head in range(2)]
    ones_lanes = [
        ((spare[head] >= runs) & (spare[head] < runs + 3)).astype(jnp.float32) for head in range(2)
    ]
    for head in range(2):
        own = in_column == spare[head]
        named = (spare[head] >= 0) & (spare[head] < runs)
        run_of[head] = own.astype(jnp.float32).astype(jnp.bfloat16)
        not_run_of[head] = (
            jnp.where(jnp.logical_and(named, jnp.logical_not(own)), NEGATIVE, 0.0) + ones_lanes[head]
        ).astype(jnp.bfloat16)

    def in_parts(head, value, rest):
        first = value.astype(jnp.bfloat16).astype(jnp.float32)
        second = (value - first).astype(jnp.bfloat16).astype(jnp.float32)
        third = value - first - second
        out = rest.astype(jnp.float32)
        for lanes, part in zip(part_lanes[head], (first, second, third)):
            out = jnp.where(lanes, part, out)
        return out.astype(jnp.bfloat16)

    def rows_of(block):
        return pl.ds(pl.multiple_of(block * BLOCK, BLOCK), BLOCK)

    def strip_of(block, strip):
        return pl.ds(pl.multiple_of(block * BLOCK + strip * STRIP, STRIP), STRIP)

    def part_copy(turn, block):
        rows = rows_of(block)
        return pltpu.make_async_remote_copy(
            parts.at[turn % 2, rows],
            landed.at[turn % 2, rows],
            part_send.at[turn, block],
            part_recv.at[turn, block],
            device_id=(dp, other),
            device_id_type=MESH,
        )

    def both_parts(turn, rows):
        return parts[turn % 2, rows, :].astype(jnp.float32) + landed[turn % 2, rows, :].astype(
            jnp.float32
        )

    def send_part(turn, block, value):
        if turn >= 2:
            part_copy(turn - 2, block).wait_send()
        parts[turn % 2, rows_of(block), :] = value.astype(jnp.bfloat16)
        part_copy(turn, block).start()

    def each(number, body, unroll=1):
        lax.fori_loop(0, number, lambda i, carry: (body(i), carry)[1], 0, unroll=unroll)

    def add_vector(place, values):
        vector_sums[place] = vector_sums[place] + column_sums(values)

    for copy in loads[:4]:
        copy.wait()
    scale = 1.0 / math.sqrt(HEAD_DIM)

    def project(block):
        rows = rows_of(block)
        got = dot(tokens[rows, :], qkv_weight[...], 1, 0)
        qkv[rows, :shard] = ((got[:, :shard] + query_bias[...]) * scale).astype(jnp.bfloat16)
        qkv[rows, shard : 2 * shard] = got[:, shard : 2 * shard].astype(jnp.bfloat16)
        qkv[rows, 2 * shard :] = (got[:, 2 * shard :] + value_bias[...]).astype(jnp.bfloat16)

    for block in range(blocks):
        project(block)

    def at(group, pair):
        start = group * shard + pair * PAIR
        return slice(start, start + PAIR)

    def attend(block):
        low, high = key_window(block, row_count)
        rows, keys, span = slice(block * BLOCK, (block + 1) * BLOCK), slice(low, high), high - low
        outs, logs = {}, {}
        slot = lambda unit: (unit % 2) * BLOCK

        def score(unit):
            pair, head = divmod(unit, 2)
            query = qkv[rows, at(0, pair)] * keep_head[head] + run_of[head, rows, :]
            key = qkv[keys, at(1, pair)] * keep_head[head] + not_run_of[head, keys, :]
            d_resid[slot(unit) : slot(unit) + BLOCK, :span] = dot(query, key, 1, 1)

        def soften(unit):
            tops = []
            for start in range(slot(unit), slot(unit) + BLOCK, STRIP):
                strip = slice(start, start + STRIP)
                scores = d_resid[strip, :span]
                tops.append(jnp.max(scores, axis=1, keepdims=True))
                grad_low[strip, :span] = jnp.exp(scores - tops[-1]).astype(jnp.bfloat16)
            logs[unit] = jnp.concatenate(tops, axis=0)

        def gather(unit):
            pair, head = divmod(unit, 2)
            value = qkv[keys, at(2, pair)] * keep_head[head] + keep_head[1 - head]
            got = dot(grad_low[slot(unit) : slot(unit) + BLOCK, :span], value, 1, 0)
            outs[unit] = got * (1.0 / pltpu.roll(got, HEAD_DIM, 1))
            logs[unit] = logs[unit] + jnp.log(got)
            if head == 1:
                context[rows, at(0, pair)] = jnp.where(
                    head_lanes, outs[unit - 1], outs[unit]
                ).astype(jnp.bfloat16)
                log_totals[pair, rows, :] = jnp.where(head_lanes, logs[unit], logs[unit - 1])

        units = 2 * pairs
        score(0)
        for unit in range(units):
            if unit + 1 < units:
                score(unit + 1)
            soften(unit)
            if unit > 0:
                gather(unit - 1)
        gather(units - 1)

    for copy in loads[4:]:
        copy.wait()
    for block in range(blocks):
        attend(block)
        if block == 0:
            pl.semaphore_wait(barrier, len(strides) + 1)
        send_part(0, block, dot(context[rows_of(block), :], output_weight[...], 1, 0))

    def normalized(values):
        centered = values - jnp.mean(values, axis=-1, keepdims=True)
        variance = jnp.mean(centered * centered, axis=-1, keepdims=True)
        inverse = lax.rsqrt(variance + EPSILON)
        return centered * inverse, inverse

    def pull_norm(grad, hat, inverse):
        return inverse * (
            grad
            - jnp.mean(grad, axis=-1, keepdims=True)
            - hat * jnp.mean(grad * hat, axis=-1, keepdims=True)
        )

    def feed_forward(block):
        part_copy(0, block).wait_recv()

        def norm(strip):
            rows = strip_of(block, strip)
            hat, inverse = normalized(
                tokens[rows, :].astype(jnp.float32) + both_parts(0, rows) + output_bias[...]
            )
            first_hat[rows, :] = hat
            row_facts[rows, 1:2] = inverse
            first_low[rows, :] = (hat * first_gain[...] + first_shift[...]).astype(jnp.bfloat16)

        each(strips, norm, 2)
        rows = rows_of(block)
        tile = hidden // 4
        for start in range(0, hidden, tile):
            some = slice(start, start + tile)
            pre = dot(first_low[rows, :], up_weight[:, some], 1, 0) + up_bias[:, some]
            below = 0.5 + 0.5 * lax.erf(pre * math.sqrt(0.5))
            density = jnp.exp(-0.5 * pre * pre) * (1.0 / math.sqrt(2.0 * math.pi))
            inner[rows, some] = (pre * below).astype(jnp.bfloat16)
            slope[rows, some] = (below + pre * density).astype(jnp.bfloat16)
        send_part(1, block, dot(inner[rows, :], down_weight[...], 1, 0))

    each(blocks, feed_forward)

    def second_norm(block):
        part_copy(1, block).wait_recv()

        def norm(strip):
            rows = strip_of(block, strip)
            first = first_hat[rows, :] * first_gain[...] + first_shift[...]
            hat, inverse = normalized(first + both_parts(1, rows) + down_bias[...])
            grad = cotangent[rows, :].astype(jnp.float32) * row_facts[rows, 0:1]
            cotangent[rows, :] = (hat * second_gain[...] + second_shift[...]).astype(jnp.bfloat16)
            back = pull_norm(grad * second_gain[...], hat, inverse)
            d_resid[rows, :] = back
            grad_low[rows, :] = back.astype(jnp.bfloat16)
            add_vector(4, grad * hat)
            add_vector(5, grad)
            add_vector(3, back)

        each(strips, norm, 2)

    each(blocks, second_norm)
    result_store = pltpu.make_async_copy(cotangent, result_hbm, store_sem.at[0])
    result_store.start()

    columns = lambda place: slice(place * shard, (place + 1) * shard)
    quarters = hidden // shard
    sources = [down_blocks.at[place] for place in range(quarters)]
    sources += [up_blocks.at[place] for place in range(quarters)]
    sources += [inner.at[:width, columns(place)] for place in range(4)]

    def total_store(c):
        return pltpu.make_async_copy(totals.at[c], sums_hbm.at[c], total_sem.at[c])

    chains = [
        Reduction(
            sources[c],
            totals.at[c],
            block_landings.at[c],
            chain_send.at[c],
            chain_recv.at[c],
            plans[c],
            dp,
            mp,
            total_store(c).start,
        )
        for c in range(count)
    ]
    chains.append(
        Reduction(
            vectors,
            vector_total,
            vector_landing,
            vector_send,
            vector_recv,
            vector_plan,
            dp,
            mp,
            lambda: None,
        )
    )
    point = iter(SCHEDULE)

    def move_chains():
        for c in next(point, ()):
            chains[c].advance()

    down_places = [(top, left) for top in range(0, hidden, width) for left in range(0, width, shard)]
    for place, (top, left) in enumerate(down_places):
        down_blocks[place] = dot(
            inner[:, top : top + width], grad_low[:, left : left + shard], 0, 0
        ).astype(jnp.bfloat16)
        move_chains()

    def through_hidden(block):
        rows = rows_of(block)
        tile = hidden // 4
        for start in range(0, hidden, tile):
            some = slice(start, start + tile)
            grad = dot(grad_low[rows, :], down_weight[some, :], 1, 1)
            low = (grad * slope[rows, some].astype(jnp.float32)).astype(jnp.bfloat16)
            d_pre[rows, some] = low
            up_bias_sums[:, some] = up_bias_sums[:, some] + column_sums(low.astype(jnp.float32))
        send_part(2, block, dot(d_pre[rows, :], up_weight[...], 1, 1))

    for block in range(blocks):
        through_hidden(block)
        move_chains()

    for place in range(quarters):
        up_blocks[place] = dot(first_low[...], d_pre[:, columns(place)], 0, 0).astype(jnp.bfloat16)
        move_chains()

    def first_norm_back(block):
        part_copy(2, block).wait_recv()

        def norm(strip):
            rows = strip_of(block, strip)
            grad = d_resid[rows, :] + both_parts(2, rows)
            hat = first_hat[rows, :]
            back = pull_norm(grad * first_gain[...], hat, row_facts[rows, 1:2])
            d_resid[rows, :] = back
            grad_low[rows, :] = back.astype(jnp.bfloat16)
            add_vector(1, grad * hat)
            add_vector(2, grad)
            add_vector(0, back)

        each(strips, norm, 2)
        rows = rows_of(block)
        d_pre[rows, :shard] = dot(grad_low[rows, :], output_weight[...], 1, 1).astype(jnp.bfloat16)

    for block in range(blocks):
        first_norm_back(block)
        move_chains()

    for start in range(0, width, shard):
        inner[start : start + shard, columns(0)] = dot(
            context[...], grad_low[:, start : start + shard], 0, 0
        ).astype(jnp.bfloat16)
    move_chains()

    first_hat[...] = jnp.zeros_like(first_hat)

    cross = (
        (lax.broadcasted_iota(jnp.int32, (PAIR, 1), 0) < HEAD_DIM) != head_lanes
    ).astype(jnp.float32)
    cross = cross.astype(jnp.bfloat16)

    def attend_back(block):
        low, high = key_window(block, row_count)
        rows = slice(block * BLOCK, (block + 1) * BLOCK)
        prepared, scored, weighed, d_queries = {}, {}, {}, {}

        def prepare(pair):
            query, grad = qkv[rows, at(0, pair)], d_pre[rows, at(0, pair)]
            product = grad.astype(jnp.float32) * context[rows, at(0, pair)].astype(jnp.float32)
            most = product.astype(jnp.bfloat16)
            rest = (product - most.astype(jnp.float32)).astype(jnp.bfloat16)
            mean = dot(most, cross, 1, 0) + dot(rest, cross, 1, 0)
            log_total = log_totals[pair, rows, :]
            prepared[pair] = []
            for head in range(2):
                own_query, own_grad = query * keep_head[head], grad * keep_head[head]
                less_log = in_parts(head, -log_total, run_of[head, rows, :])
                less_mean = in_parts(head, -mean, jnp.zeros_like(mean))
                prepared[pair].append(
                    (own_query, own_grad, own_query + less_log, own_grad + less_mean)
                )

        def score(pair, start):
            if start == low:
                prepare(pair)
            keys = slice(start, start + BLOCK)
            got = []
            for head in range(2):
                key = qkv[keys, at(1, pair)] * keep_head[head] + not_run_of[head, keys, :]
                value = qkv[keys, at(2, pair)] * keep_head[head] + ones_lanes[head].astype(
                    jnp.bfloat16
                )
                got.append(
                    (
                        dot(key, prepared[pair][head][2], 1, 1),
                        dot(value, prepared[pair][head][3], 1, 1),
                    )
                )
            scored[pair, start] = got

        def weigh(pair, start):
            got = []
            for scores, d_weights in scored.pop((pair, start)):
                weights = jnp.exp(scores)
                got.append(
                    (weights.astype(jnp.bfloat16), (weights * d_weights).astype(jnp.bfloat16))
                )
            weighed[pair, start] = got

        def gather(pair, start):
            keys = slice(start, start + BLOCK)
            key = qkv[keys, at(1, pair)]
            d_key = d_value = 0.0
            for head, (weights, d_scores) in enumerate(weighed.pop((pair, start))):
                d_value = d_value + dot(weights, prepared[pair][head][1], 1, 0)
                d_key = d_key + dot(d_scores, prepared[pair][head][0], 1, 0)
                d_query = dot(d_scores, key, 0, 0)
                d_queries[pair, head] = d_queries.get((pair, head), 0.0) + d_query
            first_hat[keys, at(0, pair)] = first_hat[keys, at(0, pair)] + d_key
            first_hat[keys, at(1, pair)] = first_hat[keys, at(1, pair)] + d_value
            if start + BLOCK == high:
                both = jnp.where(head_lanes, d_queries[pair, 0], d_queries[pair, 1])
                slope[rows, at(0, pair)] = (both * scale).astype(jnp.bfloat16)

        units = [(pair, start) for pair in range(pairs) for start in range(low, high, BLOCK)]
        score(*units[0])
        for place, unit in enumerate(units):
            if place + 1 < len(units):
                score(*units[place + 1])
            weigh(*unit)
            if place > 0:
                gather(*units[place - 1])
        gather(*units[-1])

    for block in range(blocks):
        attend_back(block)
        move_chains()

    def round_keys(strip):
        rows = pl.ds(pl.multiple_of(strip * STRIP, STRIP), STRIP)
        slope[rows, shard : 3 * shard] = first_hat[rows, :].astype(jnp.bfloat16)

    each(row_count // STRIP, round_keys, 4)

    move_chains()

    for place in range(3):
        inner[:width, columns(1 + place)] = dot(tokens[...], slope[:, columns(place)], 0, 0).astype(
            jnp.bfloat16
        )
        move_chains()

    def finish_vectors():
        for place in range(6):
            vectors[place : place + 1, :] = jnp.sum(vector_sums[place], axis=0, keepdims=True)
        up_sum = jnp.sum(up_bias_sums[...], axis=0, keepdims=True)
        for place in range(hidden // width):
            vectors[6 + place : 7 + place, :] = up_sum[:, place * width : (place + 1) * width]
        ones = jnp.ones((16, row_count), jnp.bfloat16)
        last = 6 + hidden // width
        vectors[last : last + 1, :shard] = dot(ones, slope[:, :shard], 1, 0)[:1]
        vectors[last : last + 1, shard:] = dot(ones, slope[:, 2 * shard : 3 * shard], 1, 0)[:1]

    finish_vectors()
    move_chains()

    def token_part(block):
        rows = rows_of(block)
        send_part(3, block, dot(slope[rows, : 3 * shard], qkv_weight[...], 1, 1))

    for block in range(blocks):
        token_part(block)
        move_chains()

    def tokens_back(block):
        part_copy(3, block).wait_recv()

        def total(strip):
            rows = strip_of(block, strip)
            tokens[rows, :] = (d_resid[rows, :] + both_parts(3, rows)).astype(jnp.bfloat16)

        each(strips, total, 2)

    for block in range(blocks):
        tokens_back(block)
        move_chains()
    tokens_store = pltpu.make_async_copy(tokens, tokens_grad_hbm, store_sem.at[1])
    tokens_store.start()

    move_chains()
    while any(chain.next_step <= len(chain.steps) for chain in chains):
        for chain in chains:
            chain.advance()

    for turn in (2, 3):
        for block in range(blocks):
            part_copy(turn, block).wait_send()
    result_store.wait()
    tokens_store.wait()
    for c in range(count):
        total_store(c).wait()


def widen_kernel(shard, result, tokens_grad, sums, vectors, *refs):
    (
        result_out,
        tokens_out,
        query_out,
        query_bias_out,
        key_out,
        value_out,
        value_bias_out,
        output_out,
        output_bias_out,
        first_gain_out,
        first_shift_out,
        up_out,
        up_bias_out,
        down_out,
        down_bias_out,
        second_gain_out,
        second_shift_out,
        came,
        wide,
        passing,
        pass_sem,
        load_sem,
        store_sem,
    ) = refs
    count, width = sums.shape[0], sums.shape[1]
    hidden = up_out.shape[1]
    arrays = [(result, result_out), (tokens_grad, tokens_out)]
    moves = [
        pltpu.make_async_copy(source, passing.at[i], pass_sem.at[i])
        for i, (source, target) in enumerate(arrays)
    ]
    passes = [
        pltpu.make_async_copy(passing.at[i], target, pass_sem.at[i])
        for i, (source, target) in enumerate(arrays)
    ]
    loads = [
        pltpu.make_async_copy(sums.at[c], came.at[c], load_sem.at[c]) for c in range(count)
    ]
    for copy in loads[:1] + moves + loads[1:]:
        copy.start()
    for row, out in [
        (0, output_bias_out),
        (1, first_gain_out),
        (2, first_shift_out),
        (3, down_bias_out),
        (4, second_gain_out),
        (5, second_shift_out),
    ]:
        out[...] = vectors[row]
    for place in range(hidden // width):
        up_bias_out[place * width : (place + 1) * width] = vectors[6 + place]
    last = 6 + hidden // width
    query_bias_out[...] = vectors[last, :shard]
    value_bias_out[...] = vectors[last, shard:]

    targets = [
        down_out.at[top : top + width, left : left + shard]
        for top in range(0, hidden, width)
        for left in range(0, width, shard)
    ]
    targets += [up_out.at[:, left : left + shard] for left in range(0, hidden, shard)]
    targets += [None, query_out, key_out, value_out]
    stores = []
    for c in range(count):
        loads[c].wait()
        wide[c] = came[c].astype(jnp.float32)
        if targets[c] is None:
            pieces = [
                (wide.at[c, left : left + shard], output_out.at[:, left : left + shard])
                for left in range(0, width, shard)
            ]
        else:
            pieces = [(wide.at[c], targets[c])]
        for piece, (source, target) in enumerate(pieces):
            stores.append(pltpu.make_async_copy(source, target, store_sem.at[c, piece]))
            stores[-1].start()
        if c < len(moves):
            moves[c].wait()
            passes[c].start()
    for copy in stores + passes:
        copy.wait()


SCHEDULE = [(0,), (1,), (2,), (3,), (), (), (), (), (), (), (), (), (0, 1, 4), (2,), (), (5,), (0,), (0, 1, 3, 7), (0, 1, 6, 8), (2, 3), (4, 1, 0), (), (2, 9), (), (3, 1), (0, 12), (2, 12), (5, 7, 3, 4, 12), (12,), (12,), (2,), (), (), (3, 6, 4, 1, 10, 8, 5, 7, 4, 2, 5, 9, 7, 11, 6, 5, 1, 7, 4, 3, 0, 6, 8, 5, 6, 9, 5, 8, 10, 7, 6, 4, 1, 9, 8, 11, 7, 0, 6, 10, 9, 3, 8, 9, 2, 4, 10, 5, 11, 10, 11, 10, 11, 11, 8, 3, 9, 11, 2, 4, 10, 5, 7, 6, 8, 9, 11, 7, 10, 6, 8, 9, 11, 10)]


def local(
    tokens,
    cotangent,
    lengths,
    query_weight,
    query_bias,
    key_weight,
    value_weight,
    value_bias,
    output_weight,
    output_bias,
    first_gain,
    first_shift,
    up_weight,
    up_bias,
    down_weight,
    down_bias,
    second_gain,
    second_shift,
):
    row_count, width = tokens.shape
    shard, hidden = query_weight.shape[1], up_weight.shape[1]
    dp_size = lax.axis_size("dp")
    blocks = row_count // BLOCK
    low, wide = jnp.bfloat16, jnp.float32
    count = 2 * (hidden // shard) + 4
    orders = exchange_orders(dp_size)
    plans = [plan_steps(width, orders[i % len(orders)]) for i in range(count)]
    vector_rows = ROW_TILE
    vector_plan = [(stride, vector_rows, "whole") for stride in orders[0]]
    landing = max(landing_rows(plan) for plan in plans)
    steps = max(len(plan) for plan in plans)
    hbm = pl.BlockSpec(memory_space=pl.ANY)
    vmem = pl.BlockSpec(memory_space=pltpu.VMEM)
    smem = pl.BlockSpec(memory_space=pltpu.SMEM)
    dma = pltpu.SemaphoreType.DMA
    anywhere = lambda shape, dtype: (jax.ShapeDtypeStruct(shape, dtype), hbm)
    outs = pl.pallas_call(
        functools.partial(layer_kernel, plans, vector_plan, bits_of(dp_size)),
        out_shape=[
            jax.ShapeDtypeStruct((row_count, width), low),
            jax.ShapeDtypeStruct((row_count, width), low),
            jax.ShapeDtypeStruct((count, width, shard), low),
            jax.ShapeDtypeStruct((vector_rows, width), wide),
        ],
        in_specs=[hbm, hbm, smem] + [hbm] * 6 + [vmem] * 9,
        out_specs=[hbm, hbm, hbm, vmem],
        scratch_shapes=[
            pltpu.VMEM((row_count, width), low),
            pltpu.VMEM((row_count, width), low),
            pltpu.VMEM((width, 3 * shard), low),
            pltpu.VMEM((shard, width), low),
            pltpu.VMEM((width, hidden), low),
            pltpu.VMEM((hidden, width), low),
            pltpu.VMEM((row_count, 3 * shard), low),
            pltpu.VMEM((row_count, shard), low),
            pltpu.VMEM((shard // PAIR, row_count, PAIR), wide),
            pltpu.VMEM((row_count, 2), wide),
            pltpu.VMEM((2, row_count, PAIR), low),
            pltpu.VMEM((2, row_count, PAIR), low),
            pltpu.VMEM((2, row_count, width), low),
            pltpu.VMEM((2, row_count, width), low),
            pltpu.VMEM((row_count, width), wide),
            pltpu.VMEM((row_count, width), low),
            pltpu.VMEM((row_count, hidden), low),
            pltpu.VMEM((row_count, hidden), low),
            pltpu.VMEM((row_count, hidden), low),
            pltpu.VMEM((row_count, width), wide),
            pltpu.VMEM((row_count, width), low),
            pltpu.VMEM((hidden // shard, width, shard), low),
            pltpu.VMEM((hidden // shard, width, shard), low),
            pltpu.VMEM((6, 8, width), wide),
            pltpu.VMEM((8, hidden), wide),
            pltpu.VMEM((vector_rows, width), wide),
            pltpu.VMEM((count, landing, shard), low),
            pltpu.VMEM((max(1, len(vector_plan)) * vector_rows, width), wide),
            pltpu.VMEM((count, width, shard), low),
            pltpu.VMEM((16, hidden), wide),
            dma((8,)),
            dma((2,)),
            dma((4, blocks)),
            dma((4, blocks)),
            dma((count, steps)),
            dma((count, steps)),
            dma((max(1, len(vector_plan)),)),
            dma((max(1, len(vector_plan)),)),
            dma((count,)),
        ],
        compiler_params=pltpu.CompilerParams(
            collective_id=0, has_side_effects=True, vmem_limit_bytes=63 * 2**20
        ),
        name="layer",
    )(
        tokens,
        cotangent,
        lengths,
        query_weight,
        key_weight,
        value_weight,
        output_weight,
        up_weight,
        down_weight,
        query_bias,
        value_bias,
        output_bias,
        first_gain,
        first_shift,
        up_bias,
        down_bias,
        second_gain,
        second_shift,
    )
    vector = lambda size: (jax.ShapeDtypeStruct((size,), wide), vmem)
    square = anywhere((width, shard), wide)
    shapes, specs = zip(
        anywhere((row_count, width), low),
        anywhere((row_count, width), low),
        square,
        vector(shard),
        square,
        square,
        vector(shard),
        anywhere((shard, width), wide),
        vector(width),
        vector(width),
        vector(width),
        anywhere((width, hidden), wide),
        vector(hidden),
        anywhere((hidden, width), wide),
        vector(width),
        vector(width),
        vector(width),
    )
    return pl.pallas_call(
        functools.partial(widen_kernel, shard),
        out_shape=shapes,
        in_specs=[hbm, hbm, hbm, vmem],
        out_specs=specs,
        scratch_shapes=[
            pltpu.VMEM((count, width, shard), low),
            pltpu.VMEM((count, width, shard), wide),
            pltpu.VMEM((2, row_count, width), low),
            dma((2,)),
            dma((count,)),
            dma((count, width // shard)),
        ],
        compiler_params=pltpu.CompilerParams(vmem_limit_bytes=60 * 2**20),
        name="widen",
    )(*outs)


def solution(mesh):
    in_specs = (
        P("dp", None),
        P("dp", None),
        P("dp", None),
        P(None, "mp"),
        P("mp"),
        P(None, "mp"),
        P(None, "mp"),
        P("mp"),
        P("mp", None),
        P(),
        P(),
        P(),
        P(None, "mp"),
        P("mp"),
        P("mp", None),
        P(),
        P(),
        P(),
    )
    out_specs = (
        P("dp", None),
        P("dp", None),
        P(None, "mp"),
        P("mp"),
        P(None, "mp"),
        P(None, "mp"),
        P("mp"),
        P("mp", None),
        P(),
        P(),
        P(),
        P(None, "mp"),
        P("mp"),
        P("mp", None),
        P(),
        P(),
        P(),
    )
    return jax.shard_map(local, mesh=mesh, in_specs=in_specs, out_specs=out_specs, check_vma=False)
```

```python
import functools
import math

import jax
import jax.numpy as jnp
from jax import lax
from jax.experimental import pallas as pl
from jax.experimental.pallas import tpu as pltpu
from jax.sharding import PartitionSpec as P

HEAD_DIM = 64
PAIR = 2 * HEAD_DIM
LONGEST = 200
BLOCK = 256
STRIP = 32
MESH = pl.DeviceIdType.MESH


EPSILON = 1e-12
NEGATIVE = -1e30
ROW_TILE = 16


def bits_of(count):
    bits, stride = [], 1
    while stride < count:
        bits.append(stride)
        stride *= 2
    return bits


def exchange_orders(count):
    bits = bits_of(count)
    if len(bits) < 3:
        return [bits, bits[::-1]]
    a, b, c, *rest = bits
    return [[order[0], order[1], order[2], *rest] for order in ORDERS(a, b, c)]


def ORDERS(a, b, c):
    return [
        (a, b, c),
        (b, a, c),
        (a, c, b),
        (b, c, a),
        (a, b, c),
        (b, a, c),
        (a, b, c),
        (b, a, c),
        (a, c, b),
        (b, c, a),
        (a, b, c),
        (b, a, c),
    ]


def plan_steps(rows, order):
    halvings, wholes, length = [], [], rows
    for stride in order:
        if (length // 2) % ROW_TILE == 0 and length % 2 == 0:
            length //= 2
            halvings.append((stride, length, "halve"))
        else:
            wholes.append((stride, length, "whole"))
    gathers = [(stride, sent, "gather") for stride, sent, _ in reversed(halvings)]
    return halvings + wholes + gathers


def landing_rows(steps):
    return sum(sent for _, sent, kind in steps if kind != "gather")


class Reduction:
    def __init__(self, block, total, landing, send_sem, recv_sem, steps, dp, mp, arrived):
        self.total, self.landing, self.send_sem, self.recv_sem = total, landing, send_sem, recv_sem
        self.steps, self.dp, self.mp, self.arrived = steps, dp, mp, arrived
        self.held, self.base = block, 0
        self.low, self.offset = 0, 0
        self.copies, self.next_step = [], 0

    def side(self, stride):
        return (self.dp // stride) % 2

    def advance(self):
        step = self.next_step
        if step > len(self.steps):
            return
        if step > 0:
            self.finish(step - 1)
        if step < len(self.steps):
            self.start(step)
        else:
            self.arrived()
        self.next_step += 1

    def start(self, step):
        stride, sent, kind = self.steps[step]
        side = self.side(stride)
        if kind == "gather":
            rows = pl.ds(pl.multiple_of(self.low, ROW_TILE), sent)
            source, target = self.total.at[rows], self.total.at[rows]
        else:
            start = self.base + (1 - side) * sent if kind == "halve" else self.base
            source = self.held.at[pl.ds(pl.multiple_of(start, ROW_TILE), sent)]
            target = self.landing.at[pl.ds(self.offset, sent)]
        copy = pltpu.make_async_remote_copy(
            source,
            target,
            self.send_sem.at[step],
            self.recv_sem.at[step],
            device_id=(self.dp + stride - 2 * stride * side, self.mp),
            device_id_type=MESH,
        )
        copy.start()
        self.copies.append(copy)

    def finish(self, step):
        stride, sent, kind = self.steps[step]
        side = self.side(stride)
        self.copies[step].wait()
        if kind == "gather":
            self.low = self.low - side * sent
            return
        kept = self.base + side * sent if kind == "halve" else self.base
        if kind == "halve":
            self.low = self.low + side * sent
        last = step + 1 == len(self.steps) or (
            self.steps[step + 1][2] == "gather"
        )
        held, offset, low = self.held, self.offset, self.low
        part = sent
        while part > 64 and part % 2 == 0 and (part // 2) % ROW_TILE == 0:
            part //= 2

        def add(index, carry):
            own = pl.ds(pl.multiple_of(kept + index * part, ROW_TILE), part)
            came = pl.ds(pl.multiple_of(offset + index * part, ROW_TILE), part)
            both = held[own].astype(jnp.float32) + self.landing[came].astype(jnp.float32)
            if last:
                done = pl.ds(pl.multiple_of(low + index * part, ROW_TILE), part)
                self.total[done] = both.astype(self.total.dtype)
            else:
                self.landing[came] = both.astype(self.landing.dtype)
            return carry

        lax.fori_loop(0, sent // part, add, 0)
        self.held, self.base = self.landing, offset
        self.offset += sent


def dot(left, right, left_dim, right_dim):
    return lax.dot_general(
        left, right, (((left_dim,), (right_dim,)), ((), ())), preferred_element_type=jnp.float32
    )


def column_sums(values):
    return jnp.sum(values.reshape(values.shape[0] // 8, 8, values.shape[1]), axis=0)


def key_window(block, row_count):
    low = max(0, (block * BLOCK - (LONGEST - 1)) // 128 * 128)
    high = min(row_count, -(-((block + 1) * BLOCK + LONGEST - 1) // 128) * 128)
    return low, high


def layer_kernel(
    plans,
    vector_plan,
    strides,
    tokens_hbm,
    cotangent_hbm,
    lengths,
    query_weight_hbm,
    key_weight_hbm,
    value_weight_hbm,
    output_weight_hbm,
    up_weight_hbm,
    down_weight_hbm,
    query_bias,
    value_bias,
    output_bias,
    first_gain,
    first_shift,
    up_bias,
    down_bias,
    second_gain,
    second_shift,
    result_hbm,
    tokens_grad_hbm,
    *refs,
):
    count = len(plans)
    sums_hbm, vector_total = refs[0], refs[1]
    (
        tokens,
        cotangent,
        qkv_weight,
        output_weight,
        up_weight,
        down_weight,
        qkv,
        context,
        log_totals,
        row_facts,
        run_of,
        not_run_of,
        parts,
        landed,
        first_hat,
        first_low,
        slope,
        inner,
        d_pre,
        d_resid,
        grad_low,
        down_blocks,
        up_blocks,
        vector_sums,
        up_bias_sums,
        vectors,
        block_landings,
        vector_landing,
        totals,
        bias_rows,
        load_sem,
        store_sem,
        part_send,
        part_recv,
        chain_send,
        chain_recv,
        vector_send,
        vector_recv,
        total_sem,
    ) = refs[2:]
    row_count, width = tokens.shape
    shard = context.shape[1]
    hidden = inner.shape[1]
    blocks = row_count // BLOCK
    pairs = shard // PAIR
    dp, mp = lax.axis_index("dp"), lax.axis_index("mp")
    other = 1 - mp

    barrier = pltpu.get_barrier_semaphore()
    for stride in strides:
        partner = dp + stride - 2 * stride * ((dp // stride) % 2)
        pl.semaphore_signal(barrier, inc=1, device_id=(partner, mp), device_id_type=MESH)
    pl.semaphore_signal(barrier, inc=1, device_id=(dp, other), device_id_type=MESH)

    loads = [
        pltpu.make_async_copy(source, target, load_sem.at[i])
        for i, (source, target) in enumerate(
            [
                (tokens_hbm, tokens),
                (query_weight_hbm, qkv_weight.at[:, :shard]),
                (key_weight_hbm, qkv_weight.at[:, shard : 2 * shard]),
                (value_weight_hbm, qkv_weight.at[:, 2 * shard :]),
                (output_weight_hbm, output_weight),
                (up_weight_hbm, up_weight),
                (down_weight_hbm, down_weight),
                (cotangent_hbm, cotangent),
            ]
        )
    ]
    for copy in loads[:4]:
        copy.start()

    runs = lengths.shape[1]
    column_place = lax.broadcasted_iota(jnp.int32, (row_count, 1), 0)
    in_column = jnp.zeros_like(column_place)
    end = 0
    for run in range(runs):
        end = end + lengths[0, run]
        in_column = in_column + (column_place >= end).astype(jnp.int32)
    given = [query_bias, value_bias, output_bias, first_gain, first_shift, up_bias, down_bias]
    given += [second_gain, second_shift]
    for place, vector in enumerate(given):
        bias_rows[place : place + 1, : vector.shape[0]] = vector[...].reshape(1, -1)
    query_bias, value_bias = bias_rows.at[0:1, :shard], bias_rows.at[1:2, :shard]
    output_bias, first_gain, first_shift = [bias_rows.at[i : i + 1, :width] for i in (2, 3, 4)]
    up_bias = bias_rows.at[5:6, :]
    down_bias, second_gain, second_shift = [bias_rows.at[i : i + 1, :width] for i in (6, 7, 8)]
    row_facts[:, 0:1] = (in_column < runs - 1).astype(jnp.float32)
    vector_sums[...] = jnp.zeros_like(vector_sums)
    up_bias_sums[...] = jnp.zeros_like(up_bias_sums)
    vectors[...] = jnp.zeros_like(vectors)

    lane = lax.broadcasted_iota(jnp.int32, (1, PAIR), 1)
    head_lanes = lane < HEAD_DIM
    keep_head = [
        head_lanes.astype(jnp.float32).astype(jnp.bfloat16),
        (1.0 - head_lanes.astype(jnp.float32)).astype(jnp.bfloat16),
    ]
    spare = [lane - HEAD_DIM, jnp.where(head_lanes, lane, -1)]
    part_lanes = [[spare[head] == runs + part for part in range(3)] for head in range(2)]
    ones_lanes = [
        ((spare[head] >= runs) & (spare[head] < runs + 3)).astype(jnp.float32) for head in range(2)
    ]
    for head in range(2):
        own = in_column == spare[head]
        named = (spare[head] >= 0) & (spare[head] < runs)
        run_of[head] = own.astype(jnp.float32).astype(jnp.bfloat16)
        not_run_of[head] = (
            jnp.where(jnp.logical_and(named, jnp.logical_not(own)), NEGATIVE, 0.0) + ones_lanes[head]
        ).astype(jnp.bfloat16)

    def in_parts(head, value, rest):
        first = value.astype(jnp.bfloat16).astype(jnp.float32)
        second = (value - first).astype(jnp.bfloat16).astype(jnp.float32)
        third = value - first - second
        out = rest.astype(jnp.float32)
        for lanes, part in zip(part_lanes[head], (first, second, third)):
            out = jnp.where(lanes, part, out)
        return out.astype(jnp.bfloat16)

    def rows_of(block):
        return pl.ds(pl.multiple_of(block * BLOCK, BLOCK), BLOCK)

    def part_copy(turn, block):
        rows = rows_of(block)
        return pltpu.make_async_remote_copy(
            parts.at[turn % 2, rows],
            landed.at[turn % 2, rows],
            part_send.at[turn, block],
            part_recv.at[turn, block],
            device_id=(dp, other),
            device_id_type=MESH,
        )

    def both_parts(turn, rows):
        return parts[turn % 2, rows, :].astype(jnp.float32) + landed[turn % 2, rows, :].astype(
            jnp.float32
        )

    def send_part(turn, block, value):
        if turn >= 2:
            part_copy(turn - 2, block).wait_send()
        parts[turn % 2, rows_of(block), :] = value.astype(jnp.bfloat16)
        part_copy(turn, block).start()

    def each(number, body, unroll=1):
        lax.fori_loop(0, number, lambda i, carry: (body(i), carry)[1], 0, unroll=unroll)

    def add_vector(place, values):
        vector_sums[place] = vector_sums[place] + column_sums(values)

    for copy in loads[:4]:
        copy.wait()
    for copy in loads[4:]:
        copy.start()
    scale = 1.0 / math.sqrt(HEAD_DIM)

    def project(block):
        rows = rows_of(block)
        got = dot(tokens[rows, :], qkv_weight[...], 1, 0)
        qkv[rows, :shard] = ((got[:, :shard] + query_bias[...]) * scale).astype(jnp.bfloat16)
        qkv[rows, shard : 2 * shard] = got[:, shard : 2 * shard].astype(jnp.bfloat16)
        qkv[rows, 2 * shard :] = (got[:, 2 * shard :] + value_bias[...]).astype(jnp.bfloat16)

    for block in range(blocks):
        project(block)

    def at(group, pair):
        start = group * shard + pair * PAIR
        return slice(start, start + PAIR)

    def attend(block):
        low, high = key_window(block, row_count)
        rows, keys, span = slice(block * BLOCK, (block + 1) * BLOCK), slice(low, high), high - low
        outs, logs = {}, {}
        slot = lambda unit: (unit % 2) * BLOCK

        def score(unit):
            pair, head = divmod(unit, 2)
            query = qkv[rows, at(0, pair)] * keep_head[head] + run_of[head, rows, :]
            key = qkv[keys, at(1, pair)] * keep_head[head] + not_run_of[head, keys, :]
            d_resid[slot(unit) : slot(unit) + BLOCK, :span] = dot(query, key, 1, 1)

        def soften(unit):
            tops = []
            for start in range(slot(unit), slot(unit) + BLOCK, STRIP):
                strip = slice(start, start + STRIP)
                scores = d_resid[strip, :span]
                tops.append(jnp.max(scores, axis=1, keepdims=True))
                grad_low[strip, :span] = jnp.exp(scores - tops[-1]).astype(jnp.bfloat16)
            logs[unit] = jnp.concatenate(tops, axis=0)

        def gather(unit):
            pair, head = divmod(unit, 2)
            value = qkv[keys, at(2, pair)] * keep_head[head] + keep_head[1 - head]
            got = dot(grad_low[slot(unit) : slot(unit) + BLOCK, :span], value, 1, 0)
            outs[unit] = got * (1.0 / pltpu.roll(got, HEAD_DIM, 1))
            logs[unit] = logs[unit] + jnp.log(got)
            if head == 1:
                context[rows, at(0, pair)] = jnp.where(
                    head_lanes, outs[unit - 1], outs[unit]
                ).astype(jnp.bfloat16)
                log_totals[pair, rows, :] = jnp.where(head_lanes, logs[unit], logs[unit - 1])

        units = 2 * pairs
        score(0)
        for unit in range(units):
            if unit + 1 < units:
                score(unit + 1)
            soften(unit)
            if unit > 0:
                gather(unit - 1)
        gather(units - 1)

    for block in range(blocks):
        attend(block)
        if block == 0:
            for copy in loads[4:]:
                copy.wait()
            pl.semaphore_wait(barrier, len(strides) + 1)
        send_part(0, block, dot(context[rows_of(block), :], output_weight[...], 1, 0))

    def normalized(values):
        centered = values - jnp.mean(values, axis=-1, keepdims=True)
        variance = jnp.mean(centered * centered, axis=-1, keepdims=True)
        inverse = lax.rsqrt(variance + EPSILON)
        return centered * inverse, inverse

    def pull_norm(grad, hat, inverse):
        return inverse * (
            grad
            - jnp.mean(grad, axis=-1, keepdims=True)
            - hat * jnp.mean(grad * hat, axis=-1, keepdims=True)
        )

    def first_norm(block):
        rows = rows_of(block)
        hat, inverse = normalized(
            tokens[rows, :].astype(jnp.float32) + both_parts(0, rows) + output_bias[...]
        )
        first_hat[rows, :] = hat
        row_facts[rows, 1:2] = inverse
        first_low[rows, :] = (hat * first_gain[...] + first_shift[...]).astype(jnp.bfloat16)

    tile = hidden // 4
    tiles = [slice(start, start + tile) for start in range(0, hidden, tile)]

    def hidden_units(block):
        rows = rows_of(block)
        for some in tiles:
            pre = dot(first_low[rows, :], up_weight[:, some], 1, 0) + up_bias[:, some]
            below = 0.5 + 0.5 * lax.erf(pre * math.sqrt(0.5))
            density = jnp.exp(-0.5 * pre * pre) * (1.0 / math.sqrt(2.0 * math.pi))
            inner[rows, some] = (pre * below).astype(jnp.bfloat16)
            slope[rows, some] = (below + pre * density).astype(jnp.bfloat16)

    def second_norm(block):
        rows = rows_of(block)
        first = first_hat[rows, :] * first_gain[...] + first_shift[...]
        hat, inverse = normalized(first + both_parts(1, rows) + down_bias[...])
        grad = cotangent[rows, :].astype(jnp.float32) * row_facts[rows, 0:1]
        cotangent[rows, :] = (hat * second_gain[...] + second_shift[...]).astype(jnp.bfloat16)
        back = pull_norm(grad * second_gain[...], hat, inverse)
        d_resid[rows, :] = back
        grad_low[rows, :] = back.astype(jnp.bfloat16)
        add_vector(4, grad * hat)
        add_vector(5, grad)
        add_vector(3, back)

    def through_hidden(block):
        rows = rows_of(block)
        for some in tiles:
            grad = dot(grad_low[rows, :], down_weight[some, :], 1, 1)
            low = (grad * slope[rows, some].astype(jnp.float32)).astype(jnp.bfloat16)
            d_pre[rows, some] = low
            up_bias_sums[:, some] = up_bias_sums[:, some] + column_sums(low.astype(jnp.float32))
        send_part(2, block, dot(d_pre[rows, :], up_weight[...], 1, 1))

    part_copy(0, 0).wait_recv()
    first_norm(0)
    for block in range(blocks):
        if block + 1 < blocks:
            part_copy(0, block + 1).wait_recv()
        if block >= 2:
            part_copy(1, block - 2).wait_recv()
        hidden_units(block)
        if block + 1 < blocks:
            first_norm(block + 1)
        if block >= 2:
            second_norm(block - 2)
        send_part(1, block, dot(inner[rows_of(block), :], down_weight[...], 1, 0))
    late = max(0, blocks - 2)
    for block in range(late, blocks):
        part_copy(1, block).wait_recv()
        second_norm(block)
        if block == late:
            through_hidden(0)
    result_store = pltpu.make_async_copy(cotangent, result_hbm, store_sem.at[0])
    result_store.start()

    columns = lambda place: slice(place * shard, (place + 1) * shard)
    quarters = hidden // shard
    sources = [down_blocks.at[place] for place in range(quarters)]
    sources += [up_blocks.at[place] for place in range(quarters)]
    sources += [inner.at[:width, columns(place)] for place in range(4)]

    def total_store(c):
        return pltpu.make_async_copy(totals.at[c], sums_hbm.at[c], total_sem.at[c])

    chains = [
        Reduction(
            sources[c],
            totals.at[c],
            block_landings.at[c],
            chain_send.at[c],
            chain_recv.at[c],
            plans[c],
            dp,
            mp,
            total_store(c).start,
        )
        for c in range(count)
    ]
    chains.append(
        Reduction(
            vectors,
            vector_total,
            vector_landing,
            vector_send,
            vector_recv,
            vector_plan,
            dp,
            mp,
            lambda: None,
        )
    )
    point = iter(SCHEDULE)

    def move_chains():
        for c in next(point, ()):
            chains[c].advance()

    down_places = [(top, left) for top in range(0, hidden, width) for left in range(0, width, shard)]
    for place, (top, left) in enumerate(down_places):
        down_blocks[place] = dot(
            inner[:, top : top + width], grad_low[:, left : left + shard], 0, 0
        ).astype(jnp.bfloat16)
        move_chains()

    for block in range(1, blocks):
        through_hidden(block)
        move_chains()

    def first_norm_back(block):
        rows = rows_of(block)
        grad = d_resid[rows, :] + both_parts(2, rows)
        hat = first_hat[rows, :]
        back = pull_norm(grad * first_gain[...], hat, row_facts[rows, 1:2])
        d_resid[rows, :] = back
        grad_low[rows, :] = back.astype(jnp.bfloat16)
        add_vector(1, grad * hat)
        add_vector(2, grad)
        add_vector(0, back)

    for turn in range(max(quarters, blocks)):
        if turn < blocks:
            part_copy(2, turn).wait_recv()
        if turn < quarters:
            up_blocks[turn] = dot(first_low[...], d_pre[:, columns(turn)], 0, 0).astype(
                jnp.bfloat16
            )
        if turn < blocks:
            first_norm_back(turn)
        move_chains()
    for block in range(blocks):
        rows = rows_of(block)
        d_pre[rows, :shard] = dot(grad_low[rows, :], output_weight[...], 1, 1).astype(jnp.bfloat16)

    for start in range(0, width, shard):
        inner[start : start + shard, columns(0)] = dot(
            context[...], grad_low[:, start : start + shard], 0, 0
        ).astype(jnp.bfloat16)
    move_chains()

    first_hat[...] = jnp.zeros_like(first_hat)

    cross = (
        (lax.broadcasted_iota(jnp.int32, (PAIR, 1), 0) < HEAD_DIM) != head_lanes
    ).astype(jnp.float32)
    cross = cross.astype(jnp.bfloat16)

    def attend_back(block):
        low, high = key_window(block, row_count)
        rows = slice(block * BLOCK, (block + 1) * BLOCK)
        prepared, scored, weighed, d_queries = {}, {}, {}, {}

        def prepare(pair):
            query, grad = qkv[rows, at(0, pair)], d_pre[rows, at(0, pair)]
            product = grad.astype(jnp.float32) * context[rows, at(0, pair)].astype(jnp.float32)
            most = product.astype(jnp.bfloat16)
            rest = (product - most.astype(jnp.float32)).astype(jnp.bfloat16)
            mean = dot(most, cross, 1, 0) + dot(rest, cross, 1, 0)
            log_total = log_totals[pair, rows, :]
            prepared[pair] = []
            for head in range(2):
                own_query, own_grad = query * keep_head[head], grad * keep_head[head]
                less_log = in_parts(head, -log_total, run_of[head, rows, :])
                less_mean = in_parts(head, -mean, jnp.zeros_like(mean))
                prepared[pair].append(
                    (own_query, own_grad, own_query + less_log, own_grad + less_mean)
                )

        def score(pair, start):
            if start == low:
                prepare(pair)
            keys = slice(start, start + BLOCK)
            got = []
            for head in range(2):
                key = qkv[keys, at(1, pair)] * keep_head[head] + not_run_of[head, keys, :]
                value = qkv[keys, at(2, pair)] * keep_head[head] + ones_lanes[head].astype(
                    jnp.bfloat16
                )
                got.append(
                    (
                        dot(key, prepared[pair][head][2], 1, 1),
                        dot(value, prepared[pair][head][3], 1, 1),
                    )
                )
            scored[pair, start] = got

        def weigh(pair, start):
            got = []
            for scores, d_weights in scored.pop((pair, start)):
                weights = jnp.exp(scores)
                got.append(
                    (weights.astype(jnp.bfloat16), (weights * d_weights).astype(jnp.bfloat16))
                )
            weighed[pair, start] = got

        def gather(pair, start):
            keys = slice(start, start + BLOCK)
            key = qkv[keys, at(1, pair)]
            d_key = d_value = 0.0
            for head, (weights, d_scores) in enumerate(weighed.pop((pair, start))):
                d_value = d_value + dot(weights, prepared[pair][head][1], 1, 0)
                d_key = d_key + dot(d_scores, prepared[pair][head][0], 1, 0)
                d_query = dot(d_scores, key, 0, 0)
                d_queries[pair, head] = d_queries.get((pair, head), 0.0) + d_query
            first_hat[keys, at(0, pair)] = first_hat[keys, at(0, pair)] + d_key
            first_hat[keys, at(1, pair)] = first_hat[keys, at(1, pair)] + d_value
            if start + BLOCK == high:
                both = jnp.where(head_lanes, d_queries[pair, 0], d_queries[pair, 1])
                slope[rows, at(0, pair)] = (both * scale).astype(jnp.bfloat16)

        units = [(pair, start) for pair in range(pairs) for start in range(low, high, BLOCK)]
        score(*units[0])
        for place, unit in enumerate(units):
            if place + 1 < len(units):
                score(*units[place + 1])
            weigh(*unit)
            if place > 0:
                gather(*units[place - 1])
            if unit[1] + BLOCK == high:
                move_chains()
        gather(*units[-1])

    for block in range(blocks):
        attend_back(block)

    def round_keys(strip):
        rows = pl.ds(pl.multiple_of(strip * STRIP, STRIP), STRIP)
        slope[rows, shard : 3 * shard] = first_hat[rows, :].astype(jnp.bfloat16)

    each(row_count // STRIP, round_keys, 4)

    move_chains()

    for place in range(3):
        inner[:width, columns(1 + place)] = dot(tokens[...], slope[:, columns(place)], 0, 0).astype(
            jnp.bfloat16
        )
        move_chains()

    def finish_vectors():
        for place in range(6):
            vectors[place : place + 1, :] = jnp.sum(vector_sums[place], axis=0, keepdims=True)
        up_sum = jnp.sum(up_bias_sums[...], axis=0, keepdims=True)
        for place in range(hidden // width):
            vectors[6 + place : 7 + place, :] = up_sum[:, place * width : (place + 1) * width]
        ones = jnp.ones((16, row_count), jnp.bfloat16)
        last = 6 + hidden // width
        vectors[last : last + 1, :shard] = dot(ones, slope[:, :shard], 1, 0)[:1]
        vectors[last : last + 1, shard:] = dot(ones, slope[:, 2 * shard : 3 * shard], 1, 0)[:1]

    finish_vectors()
    move_chains()

    def token_part(block):
        rows = rows_of(block)
        send_part(3, block, dot(slope[rows, : 3 * shard], qkv_weight[...], 1, 1))

    for block in range(blocks):
        token_part(block)
        move_chains()

    def tokens_back(block):
        part_copy(3, block).wait_recv()

        rows = rows_of(block)
        tokens[rows, :] = (d_resid[rows, :] + both_parts(3, rows)).astype(jnp.bfloat16)

    for block in range(blocks):
        tokens_back(block)
        move_chains()
    tokens_store = pltpu.make_async_copy(tokens, tokens_grad_hbm, store_sem.at[1])
    tokens_store.start()

    move_chains()
    while any(chain.next_step <= len(chain.steps) for chain in chains):
        for chain in chains:
            chain.advance()

    for turn in (2, 3):
        for block in range(blocks):
            part_copy(turn, block).wait_send()
    result_store.wait()
    tokens_store.wait()
    for c in range(count):
        total_store(c).wait()


def widen_kernel(shard, result, tokens_grad, sums, vectors, *refs):
    (
        result_out,
        tokens_out,
        query_out,
        query_bias_out,
        key_out,
        value_out,
        value_bias_out,
        output_out,
        output_bias_out,
        first_gain_out,
        first_shift_out,
        up_out,
        up_bias_out,
        down_out,
        down_bias_out,
        second_gain_out,
        second_shift_out,
        came,
        wide,
        passing,
        pass_sem,
        load_sem,
        store_sem,
    ) = refs
    count, width = sums.shape[0], sums.shape[1]
    hidden = up_out.shape[1]
    arrays = [(result, result_out), (tokens_grad, tokens_out)]
    moves = [
        pltpu.make_async_copy(source, passing.at[i], pass_sem.at[i])
        for i, (source, target) in enumerate(arrays)
    ]
    passes = [
        pltpu.make_async_copy(passing.at[i], target, pass_sem.at[i])
        for i, (source, target) in enumerate(arrays)
    ]
    loads = [
        pltpu.make_async_copy(sums.at[c], came.at[c], load_sem.at[c]) for c in range(count)
    ]
    for copy in loads[:1] + moves + loads[1:]:
        copy.start()
    for row, out in [
        (0, output_bias_out),
        (1, first_gain_out),
        (2, first_shift_out),
        (3, down_bias_out),
        (4, second_gain_out),
        (5, second_shift_out),
    ]:
        out[...] = vectors[row]
    for place in range(hidden // width):
        up_bias_out[place * width : (place + 1) * width] = vectors[6 + place]
    last = 6 + hidden // width
    query_bias_out[...] = vectors[last, :shard]
    value_bias_out[...] = vectors[last, shard:]

    targets = [
        down_out.at[top : top + width, left : left + shard]
        for top in range(0, hidden, width)
        for left in range(0, width, shard)
    ]
    targets += [up_out.at[:, left : left + shard] for left in range(0, hidden, shard)]
    targets += [None, query_out, key_out, value_out]
    stores = []
    for c in range(count):
        loads[c].wait()
        wide[c] = came[c].astype(jnp.float32)
        if targets[c] is None:
            pieces = [
                (wide.at[c, left : left + shard], output_out.at[:, left : left + shard])
                for left in range(0, width, shard)
            ]
        else:
            pieces = [(wide.at[c], targets[c])]
        for piece, (source, target) in enumerate(pieces):
            stores.append(pltpu.make_async_copy(source, target, store_sem.at[c, piece]))
            stores[-1].start()
        if c < len(moves):
            moves[c].wait()
            passes[c].start()
    for copy in stores + passes:
        copy.wait()


SCHEDULE = [
    (0,),
    (1,),
    (2,),
    (3,),
    (),
    (),
    (),
    (),
    (),
    (0, 1, 2, 4, 5),
    (3,),
    (),
    (2, 0, 6),
    (1,),
    (0, 7),
    (1, 2),
    (3, 4),
    (0, 1),
    (5, 8),
    (2, 0),
    (6, 3, 2),
    (1,),
    (3, 7, 5, 0),
    (4,),
    (5,),
    (3, 6, 9),
    (4,),
    (1, 0, 5, 11),
    (4, 6, 12),
    (),
    (),
    (),
    (5,),
    (4, 10),
    (),
    (),
    (6, 1, 7, 12, 3, 5, 6, 4, 0, 7, 2, 8, 12, 11, 6, 4, 10, 1, 7, 9, 7, 12, 8, 2, 3, 11, 5, 8, 10, 7, 12, 11, 4, 8, 11, 10, 9, 11, 6, 2, 8, 10, 3, 7, 11, 5, 9, 10, 8, 9, 10, 9, 11, 7, 8, 6, 9, 10, 9, 11, 8, 10, 9),
]


def local(
    tokens,
    cotangent,
    lengths,
    query_weight,
    query_bias,
    key_weight,
    value_weight,
    value_bias,
    output_weight,
    output_bias,
    first_gain,
    first_shift,
    up_weight,
    up_bias,
    down_weight,
    down_bias,
    second_gain,
    second_shift,
):
    row_count, width = tokens.shape
    shard, hidden = query_weight.shape[1], up_weight.shape[1]
    dp_size = lax.axis_size("dp")
    blocks = row_count // BLOCK
    low, wide = jnp.bfloat16, jnp.float32
    count = 2 * (hidden // shard) + 4
    orders = exchange_orders(dp_size)
    plans = [plan_steps(width, orders[i % len(orders)]) for i in range(count)]
    vector_rows = ROW_TILE
    vector_plan = [(stride, vector_rows, "whole") for stride in orders[0]]
    landing = max(landing_rows(plan) for plan in plans)
    steps = max(len(plan) for plan in plans)
    hbm = pl.BlockSpec(memory_space=pl.ANY)
    vmem = pl.BlockSpec(memory_space=pltpu.VMEM)
    smem = pl.BlockSpec(memory_space=pltpu.SMEM)
    dma = pltpu.SemaphoreType.DMA
    anywhere = lambda shape, dtype: (jax.ShapeDtypeStruct(shape, dtype), hbm)
    outs = pl.pallas_call(
        functools.partial(layer_kernel, plans, vector_plan, bits_of(dp_size)),
        out_shape=[
            jax.ShapeDtypeStruct((row_count, width), low),
            jax.ShapeDtypeStruct((row_count, width), low),
            jax.ShapeDtypeStruct((count, width, shard), low),
            jax.ShapeDtypeStruct((vector_rows, width), wide),
        ],
        in_specs=[hbm, hbm, smem] + [hbm] * 6 + [vmem] * 9,
        out_specs=[hbm, hbm, hbm, vmem],
        scratch_shapes=[
            pltpu.VMEM((row_count, width), low),
            pltpu.VMEM((row_count, width), low),
            pltpu.VMEM((width, 3 * shard), low),
            pltpu.VMEM((shard, width), low),
            pltpu.VMEM((width, hidden), low),
            pltpu.VMEM((hidden, width), low),
            pltpu.VMEM((row_count, 3 * shard), low),
            pltpu.VMEM((row_count, shard), low),
            pltpu.VMEM((shard // PAIR, row_count, PAIR), wide),
            pltpu.VMEM((row_count, 2), wide),
            pltpu.VMEM((2, row_count, PAIR), low),
            pltpu.VMEM((2, row_count, PAIR), low),
            pltpu.VMEM((2, row_count, width), low),
            pltpu.VMEM((2, row_count, width), low),
            pltpu.VMEM((row_count, width), wide),
            pltpu.VMEM((row_count, width), low),
            pltpu.VMEM((row_count, hidden), low),
            pltpu.VMEM((row_count, hidden), low),
            pltpu.VMEM((row_count, hidden), low),
            pltpu.VMEM((row_count, width), wide),
            pltpu.VMEM((row_count, width), low),
            pltpu.VMEM((hidden // shard, width, shard), low),
            pltpu.VMEM((hidden // shard, width, shard), low),
            pltpu.VMEM((6, 8, width), wide),
            pltpu.VMEM((8, hidden), wide),
            pltpu.VMEM((vector_rows, width), wide),
            pltpu.VMEM((count, landing, shard), low),
            pltpu.VMEM((max(1, len(vector_plan)) * vector_rows, width), wide),
            pltpu.VMEM((count, width, shard), low),
            pltpu.VMEM((16, hidden), wide),
            dma((8,)),
            dma((2,)),
            dma((4, blocks)),
            dma((4, blocks)),
            dma((count, steps)),
            dma((count, steps)),
            dma((max(1, len(vector_plan)),)),
            dma((max(1, len(vector_plan)),)),
            dma((count,)),
        ],
        compiler_params=pltpu.CompilerParams(
            collective_id=0, has_side_effects=True, vmem_limit_bytes=63 * 2**20
        ),
        name="layer",
    )(
        tokens,
        cotangent,
        lengths,
        query_weight,
        key_weight,
        value_weight,
        output_weight,
        up_weight,
        down_weight,
        query_bias,
        value_bias,
        output_bias,
        first_gain,
        first_shift,
        up_bias,
        down_bias,
        second_gain,
        second_shift,
    )
    vector = lambda size: (jax.ShapeDtypeStruct((size,), wide), vmem)
    square = anywhere((width, shard), wide)
    shapes, specs = zip(
        anywhere((row_count, width), low),
        anywhere((row_count, width), low),
        square,
        vector(shard),
        square,
        square,
        vector(shard),
        anywhere((shard, width), wide),
        vector(width),
        vector(width),
        vector(width),
        anywhere((width, hidden), wide),
        vector(hidden),
        anywhere((hidden, width), wide),
        vector(width),
        vector(width),
        vector(width),
    )
    return pl.pallas_call(
        functools.partial(widen_kernel, shard),
        out_shape=shapes,
        in_specs=[hbm, hbm, hbm, vmem],
        out_specs=specs,
        scratch_shapes=[
            pltpu.VMEM((count, width, shard), low),
            pltpu.VMEM((count, width, shard), wide),
            pltpu.VMEM((2, row_count, width), low),
            dma((2,)),
            dma((count,)),
            dma((count, width // shard)),
        ],
        compiler_params=pltpu.CompilerParams(vmem_limit_bytes=60 * 2**20),
        name="widen",
    )(*outs)


def solution(mesh):
    in_specs = (
        P("dp", None),
        P("dp", None),
        P("dp", None),
        P(None, "mp"),
        P("mp"),
        P(None, "mp"),
        P(None, "mp"),
        P("mp"),
        P("mp", None),
        P(),
        P(),
        P(),
        P(None, "mp"),
        P("mp"),
        P("mp", None),
        P(),
        P(),
        P(),
    )
    out_specs = (
        P("dp", None),
        P("dp", None),
        P(None, "mp"),
        P("mp"),
        P(None, "mp"),
        P(None, "mp"),
        P("mp"),
        P("mp", None),
        P(),
        P(),
        P(),
        P(None, "mp"),
        P("mp"),
        P("mp", None),
        P(),
        P(),
        P(),
    )
    return jax.shard_map(local, mesh=mesh, in_specs=in_specs, out_specs=out_specs, check_vma=False)
```

```python
import functools
import math

import jax
import jax.numpy as jnp
from jax import lax
from jax.experimental import pallas as pl
from jax.experimental.pallas import tpu as pltpu
from jax.sharding import PartitionSpec as P

HEAD_DIM = 64
PAIR = 2 * HEAD_DIM
LONGEST = 200
BLOCK = 256
STRIP = 32
MESH = pl.DeviceIdType.MESH


EPSILON = 1e-12
NEGATIVE = -1e30
ROW_TILE = 16


def bits_of(count):
    bits, stride = [], 1
    while stride < count:
        bits.append(stride)
        stride *= 2
    return bits


def exchange_orders(count):
    bits = bits_of(count)
    if len(bits) < 3:
        return [bits, bits[::-1]]
    a, b, c, *rest = bits
    return [[order[0], order[1], order[2], *rest] for order in ORDERS(a, b, c)]


def ORDERS(a, b, c):
    return [
        (a, b, c),
        (b, a, c),
        (a, c, b),
        (b, c, a),
        (a, b, c),
        (b, a, c),
        (a, b, c),
        (b, a, c),
        (a, c, b),
        (b, c, a),
        (a, b, c),
        (b, a, c),
    ]


def plan_steps(rows, order):
    halvings, wholes, length = [], [], rows
    for stride in order:
        if (length // 2) % ROW_TILE == 0 and length % 2 == 0:
            length //= 2
            halvings.append((stride, length, "halve"))
        else:
            wholes.append((stride, length, "whole"))
    gathers = [(stride, sent, "gather") for stride, sent, _ in reversed(halvings)]
    return halvings + wholes + gathers


def landing_rows(steps):
    return sum(sent for _, sent, kind in steps if kind != "gather")


class Reduction:
    def __init__(self, block, total, landing, send_sem, recv_sem, steps, dp, mp):
        self.total, self.landing, self.send_sem, self.recv_sem = total, landing, send_sem, recv_sem
        self.steps, self.dp, self.mp = steps, dp, mp
        self.held, self.base = block, 0
        self.low, self.offset = 0, 0
        self.copies, self.next_step = [], 0

    def side(self, stride):
        return (self.dp // stride) % 2

    def advance(self):
        step = self.next_step
        if step > len(self.steps):
            return
        if step > 0:
            self.finish(step - 1)
        if step < len(self.steps):
            self.start(step)
        self.next_step += 1

    def start(self, step):
        stride, sent, kind = self.steps[step]
        side = self.side(stride)
        if kind == "gather":
            rows = pl.ds(pl.multiple_of(self.low, ROW_TILE), sent)
            source, target = self.total.at[rows], self.total.at[rows]
        else:
            start = self.base + (1 - side) * sent if kind == "halve" else self.base
            source = self.held.at[pl.ds(pl.multiple_of(start, ROW_TILE), sent)]
            target = self.landing.at[pl.ds(self.offset, sent)]
        copy = pltpu.make_async_remote_copy(
            source,
            target,
            self.send_sem.at[step],
            self.recv_sem.at[step],
            device_id=(self.dp + stride - 2 * stride * side, self.mp),
            device_id_type=MESH,
        )
        copy.start()
        self.copies.append(copy)

    def finish(self, step):
        stride, sent, kind = self.steps[step]
        side = self.side(stride)
        self.copies[step].wait()
        if kind == "gather":
            self.low = self.low - side * sent
            return
        kept = self.base + side * sent if kind == "halve" else self.base
        if kind == "halve":
            self.low = self.low + side * sent
        last = step + 1 == len(self.steps) or (
            self.steps[step + 1][2] == "gather"
        )
        held, offset, low = self.held, self.offset, self.low
        part = sent
        while part > 64 and part % 2 == 0 and (part // 2) % ROW_TILE == 0:
            part //= 2

        def add(index, carry):
            own = pl.ds(pl.multiple_of(kept + index * part, ROW_TILE), part)
            came = pl.ds(pl.multiple_of(offset + index * part, ROW_TILE), part)
            both = held[own].astype(jnp.float32) + self.landing[came].astype(jnp.float32)
            if last:
                done = pl.ds(pl.multiple_of(low + index * part, ROW_TILE), part)
                self.total[done] = both.astype(self.total.dtype)
            else:
                self.landing[came] = both.astype(self.landing.dtype)
            return carry

        lax.fori_loop(0, sent // part, add, 0)
        self.held, self.base = self.landing, offset
        self.offset += sent


def dot(left, right, left_dim, right_dim):
    return lax.dot_general(
        left, right, (((left_dim,), (right_dim,)), ((), ())), preferred_element_type=jnp.float32
    )


def column_sums(values):
    return jnp.sum(values.reshape(values.shape[0] // 8, 8, values.shape[1]), axis=0)


def key_window(block, row_count):
    low = max(0, (block * BLOCK - (LONGEST - 1)) // 128 * 128)
    high = min(row_count, -(-((block + 1) * BLOCK + LONGEST - 1) // 128) * 128)
    return low, high


def layer_kernel(
    plans,
    vector_plan,
    strides,
    tokens_hbm,
    cotangent_hbm,
    lengths,
    query_weight_hbm,
    key_weight_hbm,
    value_weight_hbm,
    output_weight_hbm,
    up_weight_hbm,
    down_weight_hbm,
    query_bias,
    value_bias,
    output_bias,
    first_gain,
    first_shift,
    up_bias,
    down_bias,
    second_gain,
    second_shift,
    cotangent,
    tokens,
    totals,
    vector_total,
    *refs,
):
    count = len(plans)
    (
        qkv_weight,
        output_weight,
        up_weight,
        down_weight,
        qkv,
        context,
        log_totals,
        row_facts,
        run_of,
        not_run_of,
        parts,
        landed,
        first_hat,
        first_low,
        slope,
        inner,
        d_pre,
        d_resid,
        grad_low,
        down_blocks,
        up_blocks,
        vector_sums,
        up_bias_sums,
        vectors,
        block_landings,
        vector_landing,
        bias_rows,
        load_sem,
        part_send,
        part_recv,
        chain_send,
        chain_recv,
        vector_send,
        vector_recv,
    ) = refs
    row_count, width = tokens.shape
    shard = context.shape[1]
    hidden = inner.shape[1]
    blocks = row_count // BLOCK
    pairs = shard // PAIR
    dp, mp = lax.axis_index("dp"), lax.axis_index("mp")
    other = 1 - mp

    barrier = pltpu.get_barrier_semaphore()
    for stride in strides:
        partner = dp + stride - 2 * stride * ((dp // stride) % 2)
        pl.semaphore_signal(barrier, inc=1, device_id=(partner, mp), device_id_type=MESH)
    pl.semaphore_signal(barrier, inc=1, device_id=(dp, other), device_id_type=MESH)

    loads = [
        pltpu.make_async_copy(source, target, load_sem.at[i])
        for i, (source, target) in enumerate(
            [
                (tokens_hbm, tokens),
                (query_weight_hbm, qkv_weight.at[:, :shard]),
                (key_weight_hbm, qkv_weight.at[:, shard : 2 * shard]),
                (value_weight_hbm, qkv_weight.at[:, 2 * shard :]),
                (output_weight_hbm, output_weight),
                (up_weight_hbm, up_weight),
                (down_weight_hbm, down_weight),
                (cotangent_hbm, cotangent),
            ]
        )
    ]
    for copy in loads[:4]:
        copy.start()

    runs = lengths.shape[1]
    column_place = lax.broadcasted_iota(jnp.int32, (row_count, 1), 0)
    in_column = jnp.zeros_like(column_place)
    end = 0
    for run in range(runs):
        end = end + lengths[0, run]
        in_column = in_column + (column_place >= end).astype(jnp.int32)
    given = [query_bias, value_bias, output_bias, first_gain, first_shift, up_bias, down_bias]
    given += [second_gain, second_shift]
    for place, vector in enumerate(given):
        bias_rows[place : place + 1, : vector.shape[0]] = vector[...].reshape(1, -1)
    query_bias, value_bias = bias_rows.at[0:1, :shard], bias_rows.at[1:2, :shard]
    output_bias, first_gain, first_shift = [bias_rows.at[i : i + 1, :width] for i in (2, 3, 4)]
    up_bias = bias_rows.at[5:6, :]
    down_bias, second_gain, second_shift = [bias_rows.at[i : i + 1, :width] for i in (6, 7, 8)]
    row_facts[:, 0:1] = (in_column < runs - 1).astype(jnp.float32)
    vector_sums[...] = jnp.zeros_like(vector_sums)
    up_bias_sums[...] = jnp.zeros_like(up_bias_sums)
    vectors[...] = jnp.zeros_like(vectors)

    lane = lax.broadcasted_iota(jnp.int32, (1, PAIR), 1)
    head_lanes = lane < HEAD_DIM
    keep_head = [
        head_lanes.astype(jnp.float32).astype(jnp.bfloat16),
        (1.0 - head_lanes.astype(jnp.float32)).astype(jnp.bfloat16),
    ]
    spare = [lane - HEAD_DIM, jnp.where(head_lanes, lane, -1)]
    part_lanes = [[spare[head] == runs + part for part in range(3)] for head in range(2)]
    ones_lanes = [
        ((spare[head] >= runs) & (spare[head] < runs + 3)).astype(jnp.float32) for head in range(2)
    ]
    for head in range(2):
        own = in_column == spare[head]
        named = (spare[head] >= 0) & (spare[head] < runs)
        run_of[head] = own.astype(jnp.float32).astype(jnp.bfloat16)
        not_run_of[head] = (
            jnp.where(jnp.logical_and(named, jnp.logical_not(own)), NEGATIVE, 0.0) + ones_lanes[head]
        ).astype(jnp.bfloat16)

    def in_parts(head, value, rest):
        first = value.astype(jnp.bfloat16).astype(jnp.float32)
        second = (value - first).astype(jnp.bfloat16).astype(jnp.float32)
        third = value - first - second
        out = rest.astype(jnp.float32)
        for lanes, part in zip(part_lanes[head], (first, second, third)):
            out = jnp.where(lanes, part, out)
        return out.astype(jnp.bfloat16)

    def rows_of(block):
        return pl.ds(pl.multiple_of(block * BLOCK, BLOCK), BLOCK)

    def part_copy(turn, block):
        rows = rows_of(block)
        return pltpu.make_async_remote_copy(
            parts.at[turn % 2, rows],
            landed.at[turn % 2, rows],
            part_send.at[turn, block],
            part_recv.at[turn, block],
            device_id=(dp, other),
            device_id_type=MESH,
        )

    def both_parts(turn, rows):
        return parts[turn % 2, rows, :].astype(jnp.float32) + landed[turn % 2, rows, :].astype(
            jnp.float32
        )

    def send_part(turn, block, value):
        if turn >= 2:
            part_copy(turn - 2, block).wait_send()
        parts[turn % 2, rows_of(block), :] = value.astype(jnp.bfloat16)
        part_copy(turn, block).start()

    def each(number, body, unroll=1):
        lax.fori_loop(0, number, lambda i, carry: (body(i), carry)[1], 0, unroll=unroll)

    def add_vector(place, values):
        vector_sums[place] = vector_sums[place] + column_sums(values)

    for copy in loads[:4]:
        copy.wait()
    for copy in loads[4:]:
        copy.start()
    scale = 1.0 / math.sqrt(HEAD_DIM)

    def project(block):
        rows = rows_of(block)
        got = dot(tokens[rows, :], qkv_weight[...], 1, 0)
        qkv[rows, :shard] = ((got[:, :shard] + query_bias[...]) * scale).astype(jnp.bfloat16)
        qkv[rows, shard : 2 * shard] = got[:, shard : 2 * shard].astype(jnp.bfloat16)
        qkv[rows, 2 * shard :] = (got[:, 2 * shard :] + value_bias[...]).astype(jnp.bfloat16)

    for block in range(blocks):
        project(block)

    def at(group, pair):
        start = group * shard + pair * PAIR
        return slice(start, start + PAIR)

    def attend(block):
        low, high = key_window(block, row_count)
        rows, keys, span = slice(block * BLOCK, (block + 1) * BLOCK), slice(low, high), high - low
        outs, logs = {}, {}
        slot = lambda unit: (unit % 2) * BLOCK

        def score(unit):
            pair, head = divmod(unit, 2)
            query = qkv[rows, at(0, pair)] * keep_head[head] + run_of[head, rows, :]
            key = qkv[keys, at(1, pair)] * keep_head[head] + not_run_of[head, keys, :]
            d_resid[slot(unit) : slot(unit) + BLOCK, :span] = dot(query, key, 1, 1)

        def soften(unit):
            tops = []
            for start in range(slot(unit), slot(unit) + BLOCK, STRIP):
                strip = slice(start, start + STRIP)
                scores = d_resid[strip, :span]
                tops.append(jnp.max(scores, axis=1, keepdims=True))
                grad_low[strip, :span] = jnp.exp(scores - tops[-1]).astype(jnp.bfloat16)
            logs[unit] = jnp.concatenate(tops, axis=0)

        def gather(unit):
            pair, head = divmod(unit, 2)
            value = qkv[keys, at(2, pair)] * keep_head[head] + keep_head[1 - head]
            got = dot(grad_low[slot(unit) : slot(unit) + BLOCK, :span], value, 1, 0)
            outs[unit] = got * (1.0 / pltpu.roll(got, HEAD_DIM, 1))
            logs[unit] = logs[unit] + jnp.log(got)
            if head == 1:
                context[rows, at(0, pair)] = jnp.where(
                    head_lanes, outs[unit - 1], outs[unit]
                ).astype(jnp.bfloat16)
                log_totals[pair, rows, :] = jnp.where(head_lanes, logs[unit], logs[unit - 1])

        units = 2 * pairs
        score(0)
        for unit in range(units):
            if unit + 1 < units:
                score(unit + 1)
            soften(unit)
            if unit > 0:
                gather(unit - 1)
        gather(units - 1)

    for block in range(blocks):
        attend(block)
        if block == 0:
            for copy in loads[4:]:
                copy.wait()
            pl.semaphore_wait(barrier, len(strides) + 1)
        send_part(0, block, dot(context[rows_of(block), :], output_weight[...], 1, 0))

    def normalized(values):
        centered = values - jnp.mean(values, axis=-1, keepdims=True)
        variance = jnp.mean(centered * centered, axis=-1, keepdims=True)
        inverse = lax.rsqrt(variance + EPSILON)
        return centered * inverse, inverse

    def pull_norm(grad, hat, inverse):
        return inverse * (
            grad
            - jnp.mean(grad, axis=-1, keepdims=True)
            - hat * jnp.mean(grad * hat, axis=-1, keepdims=True)
        )

    def first_norm(block):
        rows = rows_of(block)
        hat, inverse = normalized(
            tokens[rows, :].astype(jnp.float32) + both_parts(0, rows) + output_bias[...]
        )
        first_hat[rows, :] = hat
        row_facts[rows, 1:2] = inverse
        first_low[rows, :] = (hat * first_gain[...] + first_shift[...]).astype(jnp.bfloat16)

    tile = hidden // 4
    tiles = [slice(start, start + tile) for start in range(0, hidden, tile)]

    def hidden_units(block):
        rows = rows_of(block)
        for some in tiles:
            pre = dot(first_low[rows, :], up_weight[:, some], 1, 0) + up_bias[:, some]
            below = 0.5 + 0.5 * lax.erf(pre * math.sqrt(0.5))
            density = jnp.exp(-0.5 * pre * pre) * (1.0 / math.sqrt(2.0 * math.pi))
            inner[rows, some] = (pre * below).astype(jnp.bfloat16)
            slope[rows, some] = (below + pre * density).astype(jnp.bfloat16)

    def second_norm(block):
        rows = rows_of(block)
        first = first_hat[rows, :] * first_gain[...] + first_shift[...]
        hat, inverse = normalized(first + both_parts(1, rows) + down_bias[...])
        grad = cotangent[rows, :].astype(jnp.float32) * row_facts[rows, 0:1]
        cotangent[rows, :] = (hat * second_gain[...] + second_shift[...]).astype(jnp.bfloat16)
        back = pull_norm(grad * second_gain[...], hat, inverse)
        d_resid[rows, :] = back
        grad_low[rows, :] = back.astype(jnp.bfloat16)
        add_vector(4, grad * hat)
        add_vector(5, grad)
        add_vector(3, back)

    def through_hidden(block):
        rows = rows_of(block)
        for some in tiles:
            grad = dot(grad_low[rows, :], down_weight[some, :], 1, 1)
            low = (grad * slope[rows, some].astype(jnp.float32)).astype(jnp.bfloat16)
            d_pre[rows, some] = low
            up_bias_sums[:, some] = up_bias_sums[:, some] + column_sums(low.astype(jnp.float32))
        send_part(2, block, dot(d_pre[rows, :], up_weight[...], 1, 1))

    part_copy(0, 0).wait_recv()
    first_norm(0)
    for block in range(blocks):
        if block + 1 < blocks:
            part_copy(0, block + 1).wait_recv()
        if block >= 2:
            part_copy(1, block - 2).wait_recv()
        hidden_units(block)
        if block + 1 < blocks:
            first_norm(block + 1)
        if block >= 2:
            second_norm(block - 2)
        send_part(1, block, dot(inner[rows_of(block), :], down_weight[...], 1, 0))
    late = max(0, blocks - 2)
    for block in range(late, blocks):
        part_copy(1, block).wait_recv()
        second_norm(block)
        if block == late:
            through_hidden(0)
    columns = lambda place: slice(place * shard, (place + 1) * shard)
    quarters = hidden // shard
    sources = [down_blocks.at[place] for place in range(quarters)]
    sources += [up_blocks.at[place] for place in range(quarters)]
    sources += [inner.at[:width, columns(place)] for place in range(4)]

    chains = [
        Reduction(
            sources[c],
            totals.at[c],
            block_landings.at[c],
            chain_send.at[c],
            chain_recv.at[c],
            plans[c],
            dp,
            mp,
        )
        for c in range(count)
    ]
    chains.append(
        Reduction(
            vectors,
            vector_total,
            vector_landing,
            vector_send,
            vector_recv,
            vector_plan,
            dp,
            mp,
        )
    )
    point = iter(SCHEDULE)

    def move_chains():
        for c in next(point, ()):
            chains[c].advance()

    down_places = [(top, left) for top in range(0, hidden, width) for left in range(0, width, shard)]
    for place, (top, left) in enumerate(down_places):
        down_blocks[place] = dot(
            inner[:, top : top + width], grad_low[:, left : left + shard], 0, 0
        ).astype(jnp.bfloat16)
        move_chains()

    for block in range(1, blocks):
        through_hidden(block)
        move_chains()

    def first_norm_back(block):
        rows = rows_of(block)
        grad = d_resid[rows, :] + both_parts(2, rows)
        hat = first_hat[rows, :]
        back = pull_norm(grad * first_gain[...], hat, row_facts[rows, 1:2])
        d_resid[rows, :] = back
        grad_low[rows, :] = back.astype(jnp.bfloat16)
        add_vector(1, grad * hat)
        add_vector(2, grad)
        add_vector(0, back)

    for turn in range(max(quarters, blocks)):
        if turn < blocks:
            part_copy(2, turn).wait_recv()
        if turn < quarters:
            up_blocks[turn] = dot(first_low[...], d_pre[:, columns(turn)], 0, 0).astype(
                jnp.bfloat16
            )
        if turn < blocks:
            first_norm_back(turn)
        move_chains()
    for block in range(blocks):
        rows = rows_of(block)
        d_pre[rows, :shard] = dot(grad_low[rows, :], output_weight[...], 1, 1).astype(jnp.bfloat16)

    for start in range(0, width, shard):
        inner[start : start + shard, columns(0)] = dot(
            context[...], grad_low[:, start : start + shard], 0, 0
        ).astype(jnp.bfloat16)
    move_chains()

    first_hat[...] = jnp.zeros_like(first_hat)

    cross = (
        (lax.broadcasted_iota(jnp.int32, (PAIR, 1), 0) < HEAD_DIM) != head_lanes
    ).astype(jnp.float32)
    cross = cross.astype(jnp.bfloat16)

    def attend_back(block):
        low, high = key_window(block, row_count)
        rows = slice(block * BLOCK, (block + 1) * BLOCK)
        prepared, scored, weighed, d_queries = {}, {}, {}, {}

        def prepare(pair):
            query, grad = qkv[rows, at(0, pair)], d_pre[rows, at(0, pair)]
            product = grad.astype(jnp.float32) * context[rows, at(0, pair)].astype(jnp.float32)
            most = product.astype(jnp.bfloat16)
            rest = (product - most.astype(jnp.float32)).astype(jnp.bfloat16)
            mean = dot(most, cross, 1, 0) + dot(rest, cross, 1, 0)
            log_total = log_totals[pair, rows, :]
            prepared[pair] = []
            for head in range(2):
                own_query, own_grad = query * keep_head[head], grad * keep_head[head]
                less_log = in_parts(head, -log_total, run_of[head, rows, :])
                less_mean = in_parts(head, -mean, jnp.zeros_like(mean))
                prepared[pair].append(
                    (own_query, own_grad, own_query + less_log, own_grad + less_mean)
                )

        def score(pair, start):
            if start == low:
                prepare(pair)
            keys = slice(start, start + BLOCK)
            got = []
            for head in range(2):
                key = qkv[keys, at(1, pair)] * keep_head[head] + not_run_of[head, keys, :]
                value = qkv[keys, at(2, pair)] * keep_head[head] + ones_lanes[head].astype(
                    jnp.bfloat16
                )
                got.append(
                    (
                        dot(key, prepared[pair][head][2], 1, 1),
                        dot(value, prepared[pair][head][3], 1, 1),
                    )
                )
            scored[pair, start] = got

        def weigh(pair, start):
            got = []
            for scores, d_weights in scored.pop((pair, start)):
                weights = jnp.exp(scores)
                got.append(
                    (weights.astype(jnp.bfloat16), (weights * d_weights).astype(jnp.bfloat16))
                )
            weighed[pair, start] = got

        def gather(pair, start):
            keys = slice(start, start + BLOCK)
            key = qkv[keys, at(1, pair)]
            d_key = d_value = 0.0
            for head, (weights, d_scores) in enumerate(weighed.pop((pair, start))):
                d_value = d_value + dot(weights, prepared[pair][head][1], 1, 0)
                d_key = d_key + dot(d_scores, prepared[pair][head][0], 1, 0)
                d_query = dot(d_scores, key, 0, 0)
                d_queries[pair, head] = d_queries.get((pair, head), 0.0) + d_query
            first_hat[keys, at(0, pair)] = first_hat[keys, at(0, pair)] + d_key
            first_hat[keys, at(1, pair)] = first_hat[keys, at(1, pair)] + d_value
            if start + BLOCK == high:
                both = jnp.where(head_lanes, d_queries[pair, 0], d_queries[pair, 1])
                slope[rows, at(0, pair)] = (both * scale).astype(jnp.bfloat16)

        units = [(pair, start) for pair in range(pairs) for start in range(low, high, BLOCK)]
        score(*units[0])
        for place, unit in enumerate(units):
            if place + 1 < len(units):
                score(*units[place + 1])
            weigh(*unit)
            if place > 0:
                gather(*units[place - 1])
            if unit[1] + BLOCK == high:
                move_chains()
        gather(*units[-1])

    for block in range(blocks):
        attend_back(block)

    def round_keys(strip):
        rows = pl.ds(pl.multiple_of(strip * STRIP, STRIP), STRIP)
        slope[rows, shard : 3 * shard] = first_hat[rows, :].astype(jnp.bfloat16)

    each(row_count // STRIP, round_keys, 4)

    move_chains()

    for place in range(3):
        inner[:width, columns(1 + place)] = dot(tokens[...], slope[:, columns(place)], 0, 0).astype(
            jnp.bfloat16
        )
        move_chains()

    def finish_vectors():
        for place in range(6):
            vectors[place : place + 1, :] = jnp.sum(vector_sums[place], axis=0, keepdims=True)
        up_sum = jnp.sum(up_bias_sums[...], axis=0, keepdims=True)
        for place in range(hidden // width):
            vectors[6 + place : 7 + place, :] = up_sum[:, place * width : (place + 1) * width]
        ones = jnp.ones((16, row_count), jnp.bfloat16)
        last = 6 + hidden // width
        vectors[last : last + 1, :shard] = dot(ones, slope[:, :shard], 1, 0)[:1]
        vectors[last : last + 1, shard:] = dot(ones, slope[:, 2 * shard : 3 * shard], 1, 0)[:1]

    finish_vectors()
    move_chains()

    def token_part(block):
        rows = rows_of(block)
        send_part(3, block, dot(slope[rows, : 3 * shard], qkv_weight[...], 1, 1))

    for block in range(blocks):
        token_part(block)
        move_chains()

    def tokens_back(block):
        part_copy(3, block).wait_recv()

        rows = rows_of(block)
        tokens[rows, :] = (d_resid[rows, :] + both_parts(3, rows)).astype(jnp.bfloat16)

    for block in range(blocks):
        tokens_back(block)
        move_chains()

    move_chains()
    while any(chain.next_step <= len(chain.steps) for chain in chains):
        for chain in chains:
            chain.advance()

    for turn in (2, 3):
        for block in range(blocks):
            part_copy(turn, block).wait_send()


def widen_kernel(shard, result, tokens_grad, sums, vectors, *refs):
    (
        result_out,
        tokens_out,
        query_out,
        query_bias_out,
        key_out,
        value_out,
        value_bias_out,
        output_out,
        output_bias_out,
        first_gain_out,
        first_shift_out,
        up_out,
        up_bias_out,
        down_out,
        down_bias_out,
        second_gain_out,
        second_shift_out,
        wide,
        pass_sem,
        store_sem,
    ) = refs
    count, width = sums.shape[0], sums.shape[1]
    hidden = up_out.shape[1]
    passes = [
        pltpu.make_async_copy(source, target, pass_sem.at[i])
        for i, (source, target) in enumerate([(result, result_out), (tokens_grad, tokens_out)])
    ]
    for copy in passes:
        copy.start()
    for row, out in [
        (0, output_bias_out),
        (1, first_gain_out),
        (2, first_shift_out),
        (3, down_bias_out),
        (4, second_gain_out),
        (5, second_shift_out),
    ]:
        out[...] = vectors[row]
    for place in range(hidden // width):
        up_bias_out[place * width : (place + 1) * width] = vectors[6 + place]
    last = 6 + hidden // width
    query_bias_out[...] = vectors[last, :shard]
    value_bias_out[...] = vectors[last, shard:]

    targets = [
        down_out.at[top : top + width, left : left + shard]
        for top in range(0, hidden, width)
        for left in range(0, width, shard)
    ]
    targets += [up_out.at[:, left : left + shard] for left in range(0, hidden, shard)]
    targets += [None, query_out, key_out, value_out]
    stores = []
    for c in range(count):
        wide[c] = sums[c].astype(jnp.float32)
        if targets[c] is None:
            pieces = [
                (wide.at[c, left : left + shard], output_out.at[:, left : left + shard])
                for left in range(0, width, shard)
            ]
        else:
            pieces = [(wide.at[c], targets[c])]
        for piece, (source, target) in enumerate(pieces):
            stores.append(pltpu.make_async_copy(source, target, store_sem.at[c, piece]))
            stores[-1].start()
    for copy in stores + passes:
        copy.wait()


SCHEDULE = [
    (0,),
    (1,),
    (2,),
    (3,),
    (),
    (),
    (),
    (),
    (),
    (0, 1, 2, 4, 5),
    (3,),
    (),
    (2, 0, 6),
    (1,),
    (0, 7),
    (1, 2),
    (3, 4),
    (0, 1),
    (5, 8),
    (2, 0),
    (6, 3, 2),
    (1,),
    (3, 7, 5, 0),
    (4,),
    (5,),
    (3, 6, 9),
    (4,),
    (1, 0, 5, 11),
    (4, 6, 12),
    (),
    (),
    (),
    (5,),
    (4, 10),
    (),
    (),
    (6, 1, 7, 12, 3, 5, 6, 4, 0, 7, 2, 8, 12, 11, 6, 4, 10, 1, 7, 9, 7, 12, 8, 2, 3, 11, 5, 8, 10, 7, 12, 11, 4, 8, 11, 10, 9, 11, 6, 2, 8, 10, 3, 7, 11, 5, 9, 10, 8, 9, 10, 9, 11, 7, 8, 6, 9, 10, 9, 11, 8, 10, 9),
]


def local(
    tokens,
    cotangent,
    lengths,
    query_weight,
    query_bias,
    key_weight,
    value_weight,
    value_bias,
    output_weight,
    output_bias,
    first_gain,
    first_shift,
    up_weight,
    up_bias,
    down_weight,
    down_bias,
    second_gain,
    second_shift,
):
    row_count, width = tokens.shape
    shard, hidden = query_weight.shape[1], up_weight.shape[1]
    dp_size = lax.axis_size("dp")
    blocks = row_count // BLOCK
    low, wide = jnp.bfloat16, jnp.float32
    count = 2 * (hidden // shard) + 4
    orders = exchange_orders(dp_size)
    plans = [plan_steps(width, orders[i % len(orders)]) for i in range(count)]
    vector_rows = ROW_TILE
    vector_plan = [(stride, vector_rows, "whole") for stride in orders[0]]
    landing = max(landing_rows(plan) for plan in plans)
    steps = max(len(plan) for plan in plans)
    hbm = pl.BlockSpec(memory_space=pl.ANY)
    vmem = pl.BlockSpec(memory_space=pltpu.VMEM)
    smem = pl.BlockSpec(memory_space=pltpu.SMEM)
    dma = pltpu.SemaphoreType.DMA
    anywhere = lambda shape, dtype: (jax.ShapeDtypeStruct(shape, dtype), hbm)
    outs = pl.pallas_call(
        functools.partial(layer_kernel, plans, vector_plan, bits_of(dp_size)),
        out_shape=[
            pltpu.VMEM((row_count, width), low),
            pltpu.VMEM((row_count, width), low),
            pltpu.VMEM((count, width, shard), low),
            pltpu.VMEM((vector_rows, width), wide),
        ],
        in_specs=[hbm, hbm, smem] + [hbm] * 6 + [vmem] * 9,
        out_specs=[vmem] * 4,
        scratch_shapes=[
            pltpu.VMEM((width, 3 * shard), low),
            pltpu.VMEM((shard, width), low),
            pltpu.VMEM((width, hidden), low),
            pltpu.VMEM((hidden, width), low),
            pltpu.VMEM((row_count, 3 * shard), low),
            pltpu.VMEM((row_count, shard), low),
            pltpu.VMEM((shard // PAIR, row_count, PAIR), wide),
            pltpu.VMEM((row_count, 2), wide),
            pltpu.VMEM((2, row_count, PAIR), low),
            pltpu.VMEM((2, row_count, PAIR), low),
            pltpu.VMEM((2, row_count, width), low),
            pltpu.VMEM((2, row_count, width), low),
            pltpu.VMEM((row_count, width), wide),
            pltpu.VMEM((row_count, width), low),
            pltpu.VMEM((row_count, hidden), low),
            pltpu.VMEM((row_count, hidden), low),
            pltpu.VMEM((row_count, hidden), low),
            pltpu.VMEM((row_count, width), wide),
            pltpu.VMEM((row_count, width), low),
            pltpu.VMEM((hidden // shard, width, shard), low),
            pltpu.VMEM((hidden // shard, width, shard), low),
            pltpu.VMEM((6, 8, width), wide),
            pltpu.VMEM((8, hidden), wide),
            pltpu.VMEM((vector_rows, width), wide),
            pltpu.VMEM((count, landing, shard), low),
            pltpu.VMEM((max(1, len(vector_plan)) * vector_rows, width), wide),
            pltpu.VMEM((16, hidden), wide),
            dma((8,)),
            dma((4, blocks)),
            dma((4, blocks)),
            dma((count, steps)),
            dma((count, steps)),
            dma((max(1, len(vector_plan)),)),
            dma((max(1, len(vector_plan)),)),
        ],
        compiler_params=pltpu.CompilerParams(
            collective_id=0, has_side_effects=True, vmem_limit_bytes=54 * 2**20
        ),
        name="layer",
    )(
        tokens,
        cotangent,
        lengths,
        query_weight,
        key_weight,
        value_weight,
        output_weight,
        up_weight,
        down_weight,
        query_bias,
        value_bias,
        output_bias,
        first_gain,
        first_shift,
        up_bias,
        down_bias,
        second_gain,
        second_shift,
    )
    vector = lambda size: (jax.ShapeDtypeStruct((size,), wide), vmem)
    square = anywhere((width, shard), wide)
    shapes, specs = zip(
        anywhere((row_count, width), low),
        anywhere((row_count, width), low),
        square,
        vector(shard),
        square,
        square,
        vector(shard),
        anywhere((shard, width), wide),
        vector(width),
        vector(width),
        vector(width),
        anywhere((width, hidden), wide),
        vector(hidden),
        anywhere((hidden, width), wide),
        vector(width),
        vector(width),
        vector(width),
    )
    return pl.pallas_call(
        functools.partial(widen_kernel, shard),
        out_shape=shapes,
        in_specs=[vmem] * 4,
        out_specs=specs,
        scratch_shapes=[
            pltpu.VMEM((count, width, shard), wide),
            dma((2,)),
            dma((count, width // shard)),
        ],
        compiler_params=pltpu.CompilerParams(vmem_limit_bytes=20 * 2**20),
        name="widen",
    )(*outs)


def solution(mesh):
    in_specs = (
        P("dp", None),
        P("dp", None),
        P("dp", None),
        P(None, "mp"),
        P("mp"),
        P(None, "mp"),
        P(None, "mp"),
        P("mp"),
        P("mp", None),
        P(),
        P(),
        P(),
        P(None, "mp"),
        P("mp"),
        P("mp", None),
        P(),
        P(),
        P(),
    )
    out_specs = (
        P("dp", None),
        P("dp", None),
        P(None, "mp"),
        P("mp"),
        P(None, "mp"),
        P(None, "mp"),
        P("mp"),
        P("mp", None),
        P(),
        P(),
        P(),
        P(None, "mp"),
        P("mp"),
        P("mp", None),
        P(),
        P(),
        P(),
    )
    return jax.shard_map(local, mesh=mesh, in_specs=in_specs, out_specs=out_specs, check_vma=False)
```

```python
import functools
import math

import jax
import jax.numpy as jnp
from jax import lax
from jax.experimental import pallas as pl
from jax.experimental.pallas import tpu as pltpu
from jax.sharding import PartitionSpec as P

HEAD_DIM = 64
PAIR = 2 * HEAD_DIM
LONGEST = 200
BLOCK = 256
STRIP = 32
MESH = pl.DeviceIdType.MESH


EPSILON = 1e-12
NEGATIVE = -1e30
ROW_TILE = 16


def bits_of(count):
    bits, stride = [], 1
    while stride < count:
        bits.append(stride)
        stride *= 2
    return bits


def exchange_orders(count):
    bits = bits_of(count)
    if len(bits) < 3:
        return [bits, bits[::-1]]
    a, b, c, *rest = bits
    return [[order[0], order[1], order[2], *rest] for order in ORDERS(a, b, c)]


def ORDERS(a, b, c):
    return [
        (a, b, c),
        (b, a, c),
        (a, c, b),
        (b, c, a),
        (a, b, c),
        (b, a, c),
        (a, b, c),
        (b, a, c),
        (a, c, b),
        (b, c, a),
        (a, b, c),
        (b, a, c),
    ]


def plan_steps(rows, order):
    halvings, wholes, length = [], [], rows
    for stride in order:
        if (length // 2) % ROW_TILE == 0 and length % 2 == 0:
            length //= 2
            halvings.append((stride, length, "halve"))
        else:
            wholes.append((stride, length, "whole"))
    gathers = [(stride, sent, "gather") for stride, sent, _ in reversed(halvings)]
    return halvings + wholes + gathers


def landing_rows(steps):
    return sum(sent for _, sent, kind in steps if kind != "gather")


class Reduction:
    def __init__(self, block, total, landing, send_sem, recv_sem, steps, dp, mp):
        self.total, self.landing, self.send_sem, self.recv_sem = total, landing, send_sem, recv_sem
        self.steps, self.dp, self.mp = steps, dp, mp
        self.held, self.base = block, 0
        self.low, self.offset = 0, 0
        self.copies, self.next_step = [], 0

    def side(self, stride):
        return (self.dp // stride) % 2

    def advance(self):
        step = self.next_step
        if step > len(self.steps):
            return
        if step > 0:
            self.finish(step - 1)
        if step < len(self.steps):
            self.start(step)
        self.next_step += 1

    def start(self, step):
        stride, sent, kind = self.steps[step]
        side = self.side(stride)
        if kind == "gather":
            rows = pl.ds(pl.multiple_of(self.low, ROW_TILE), sent)
            source, target = self.total.at[rows], self.total.at[rows]
        else:
            start = self.base + (1 - side) * sent if kind == "halve" else self.base
            source = self.held.at[pl.ds(pl.multiple_of(start, ROW_TILE), sent)]
            target = self.landing.at[pl.ds(self.offset, sent)]
        copy = pltpu.make_async_remote_copy(
            source,
            target,
            self.send_sem.at[step],
            self.recv_sem.at[step],
            device_id=(self.dp + stride - 2 * stride * side, self.mp),
            device_id_type=MESH,
        )
        copy.start()
        self.copies.append(copy)

    def finish(self, step):
        stride, sent, kind = self.steps[step]
        side = self.side(stride)
        self.copies[step].wait()
        if kind == "gather":
            self.low = self.low - side * sent
            return
        kept = self.base + side * sent if kind == "halve" else self.base
        if kind == "halve":
            self.low = self.low + side * sent
        last = step + 1 == len(self.steps) or (
            self.steps[step + 1][2] == "gather"
        )
        held, offset, low = self.held, self.offset, self.low
        part = sent
        while part > 200 and part % 2 == 0 and (part // 2) % ROW_TILE == 0:
            part //= 2

        def add(index, carry):
            own = pl.ds(pl.multiple_of(kept + index * part, ROW_TILE), part)
            came = pl.ds(pl.multiple_of(offset + index * part, ROW_TILE), part)
            both = held[own].astype(jnp.float32) + self.landing[came].astype(jnp.float32)
            if last:
                done = pl.ds(pl.multiple_of(low + index * part, ROW_TILE), part)
                self.total[done] = both.astype(self.total.dtype)
            else:
                self.landing[came] = both.astype(self.landing.dtype)
            return carry

        lax.fori_loop(0, sent // part, add, 0)
        self.held, self.base = self.landing, offset
        self.offset += sent


def dot(left, right, left_dim, right_dim):
    return lax.dot_general(
        left, right, (((left_dim,), (right_dim,)), ((), ())), preferred_element_type=jnp.float32
    )


def column_sums(values):
    return jnp.sum(values.reshape(values.shape[0] // 8, 8, values.shape[1]), axis=0)


def key_window(block, row_count):
    low = max(0, (block * BLOCK - (LONGEST - 1)) // 128 * 128)
    high = min(row_count, -(-((block + 1) * BLOCK + LONGEST - 1) // 128) * 128)
    return low, high


def layer_kernel(
    plans,
    vector_plan,
    strides,
    tokens_hbm,
    cotangent_hbm,
    lengths,
    query_weight_hbm,
    key_weight_hbm,
    value_weight_hbm,
    output_weight_hbm,
    up_weight_hbm,
    down_weight_hbm,
    query_bias,
    value_bias,
    output_bias,
    first_gain,
    first_shift,
    up_bias,
    down_bias,
    second_gain,
    second_shift,
    cotangent,
    tokens,
    totals,
    vector_total,
    *refs,
):
    count = len(plans)
    (
        qkv_weight,
        output_weight,
        up_weight,
        down_weight,
        qkv,
        context,
        log_totals,
        row_facts,
        run_of,
        not_run_of,
        parts,
        landed,
        first_hat,
        first_low,
        slope,
        inner,
        d_pre,
        d_resid,
        grad_low,
        down_blocks,
        up_blocks,
        vector_sums,
        up_bias_sums,
        vectors,
        block_landings,
        vector_landing,
        bias_rows,
        load_sem,
        part_send,
        part_recv,
        chain_send,
        chain_recv,
        vector_send,
        vector_recv,
    ) = refs
    row_count, width = tokens.shape
    shard = context.shape[1]
    hidden = inner.shape[1]
    blocks = row_count // BLOCK
    pairs = shard // PAIR
    dp, mp = lax.axis_index("dp"), lax.axis_index("mp")
    other = 1 - mp

    barrier = pltpu.get_barrier_semaphore()
    for stride in strides:
        partner = dp + stride - 2 * stride * ((dp // stride) % 2)
        pl.semaphore_signal(barrier, inc=1, device_id=(partner, mp), device_id_type=MESH)
    pl.semaphore_signal(barrier, inc=1, device_id=(dp, other), device_id_type=MESH)

    loads = [
        pltpu.make_async_copy(source, target, load_sem.at[i])
        for i, (source, target) in enumerate(
            [
                (tokens_hbm, tokens),
                (query_weight_hbm, qkv_weight.at[:, :shard]),
                (key_weight_hbm, qkv_weight.at[:, shard : 2 * shard]),
                (value_weight_hbm, qkv_weight.at[:, 2 * shard :]),
                (output_weight_hbm, output_weight),
                (up_weight_hbm, up_weight),
                (down_weight_hbm, down_weight),
                (cotangent_hbm, cotangent),
            ]
        )
    ]
    for copy in loads[:4]:
        copy.start()

    runs = lengths.shape[1]
    column_place = lax.broadcasted_iota(jnp.int32, (row_count, 1), 0)
    in_column = jnp.zeros_like(column_place)
    end = 0
    for run in range(runs):
        end = end + lengths[0, run]
        in_column = in_column + (column_place >= end).astype(jnp.int32)
    given = [query_bias, value_bias, output_bias, first_gain, first_shift, up_bias, down_bias]
    given += [second_gain, second_shift]
    for place, vector in enumerate(given):
        bias_rows[place : place + 1, : vector.shape[0]] = vector[...].reshape(1, -1)
    query_bias, value_bias = bias_rows.at[0:1, :shard], bias_rows.at[1:2, :shard]
    output_bias, first_gain, first_shift = [bias_rows.at[i : i + 1, :width] for i in (2, 3, 4)]
    up_bias = bias_rows.at[5:6, :]
    down_bias, second_gain, second_shift = [bias_rows.at[i : i + 1, :width] for i in (6, 7, 8)]
    row_facts[:, 0:1] = (in_column < runs - 1).astype(jnp.float32)
    vector_sums[...] = jnp.zeros_like(vector_sums)
    up_bias_sums[...] = jnp.zeros_like(up_bias_sums)
    vectors[...] = jnp.zeros_like(vectors)

    lane = lax.broadcasted_iota(jnp.int32, (1, PAIR), 1)
    head_lanes = lane < HEAD_DIM
    keep_head = [
        head_lanes.astype(jnp.float32).astype(jnp.bfloat16),
        (1.0 - head_lanes.astype(jnp.float32)).astype(jnp.bfloat16),
    ]
    spare = [lane - HEAD_DIM, jnp.where(head_lanes, lane, -1)]
    part_lanes = [[spare[head] == runs + part for part in range(3)] for head in range(2)]
    ones_lanes = [
        ((spare[head] >= runs) & (spare[head] < runs + 3)).astype(jnp.float32) for head in range(2)
    ]
    for head in range(2):
        own = in_column == spare[head]
        named = (spare[head] >= 0) & (spare[head] < runs)
        run_of[head] = own.astype(jnp.float32).astype(jnp.bfloat16)
        not_run_of[head] = (
            jnp.where(jnp.logical_and(named, jnp.logical_not(own)), NEGATIVE, 0.0) + ones_lanes[head]
        ).astype(jnp.bfloat16)

    def in_parts(head, value, rest):
        first = value.astype(jnp.bfloat16).astype(jnp.float32)
        second = (value - first).astype(jnp.bfloat16).astype(jnp.float32)
        third = value - first - second
        out = rest.astype(jnp.float32)
        for lanes, part in zip(part_lanes[head], (first, second, third)):
            out = jnp.where(lanes, part, out)
        return out.astype(jnp.bfloat16)

    def rows_of(block):
        return pl.ds(pl.multiple_of(block * BLOCK, BLOCK), BLOCK)

    def part_copy(turn, block):
        rows = rows_of(block)
        return pltpu.make_async_remote_copy(
            parts.at[turn % 2, rows],
            landed.at[turn % 2, rows],
            part_send.at[turn, block],
            part_recv.at[turn, block],
            device_id=(dp, other),
            device_id_type=MESH,
        )

    def both_parts(turn, rows):
        return parts[turn % 2, rows, :].astype(jnp.float32) + landed[turn % 2, rows, :].astype(
            jnp.float32
        )

    def send_part(turn, block, value):
        if turn >= 2:
            part_copy(turn - 2, block).wait_send()
        parts[turn % 2, rows_of(block), :] = value.astype(jnp.bfloat16)
        part_copy(turn, block).start()

    def each(number, body, unroll=1):
        lax.fori_loop(0, number, lambda i, carry: (body(i), carry)[1], 0, unroll=unroll)

    def add_vector(place, values):
        vector_sums[place] = vector_sums[place] + column_sums(values)

    for copy in loads[:4]:
        copy.wait()
    for copy in loads[4:]:
        copy.start()
    scale = 1.0 / math.sqrt(HEAD_DIM)

    def project(block):
        rows = rows_of(block)
        got = dot(tokens[rows, :], qkv_weight[...], 1, 0)
        qkv[rows, :shard] = ((got[:, :shard] + query_bias[...]) * scale).astype(jnp.bfloat16)
        qkv[rows, shard : 2 * shard] = got[:, shard : 2 * shard].astype(jnp.bfloat16)
        qkv[rows, 2 * shard :] = (got[:, 2 * shard :] + value_bias[...]).astype(jnp.bfloat16)

    for block in range(blocks):
        project(block)

    def at(group, pair):
        start = group * shard + pair * PAIR
        return slice(start, start + PAIR)

    def attend(block):
        low, high = key_window(block, row_count)
        rows, keys, span = slice(block * BLOCK, (block + 1) * BLOCK), slice(low, high), high - low
        outs, logs = {}, {}
        slot = lambda unit: (unit % 2) * BLOCK

        def score(unit):
            pair, head = divmod(unit, 2)
            query = qkv[rows, at(0, pair)] * keep_head[head] + run_of[head, rows, :]
            key = qkv[keys, at(1, pair)] * keep_head[head] + not_run_of[head, keys, :]
            d_resid[slot(unit) : slot(unit) + BLOCK, :span] = dot(query, key, 1, 1)

        def soften(unit):
            tops = []
            for start in range(slot(unit), slot(unit) + BLOCK, STRIP):
                strip = slice(start, start + STRIP)
                scores = d_resid[strip, :span]
                tops.append(jnp.max(scores, axis=1, keepdims=True))
                grad_low[strip, :span] = jnp.exp(scores - tops[-1]).astype(jnp.bfloat16)
            logs[unit] = jnp.concatenate(tops, axis=0)

        def gather(unit):
            pair, head = divmod(unit, 2)
            value = qkv[keys, at(2, pair)] * keep_head[head] + keep_head[1 - head]
            got = dot(grad_low[slot(unit) : slot(unit) + BLOCK, :span], value, 1, 0)
            outs[unit] = got * (1.0 / pltpu.roll(got, HEAD_DIM, 1))
            logs[unit] = logs[unit] + jnp.log(got)
            if head == 1:
                context[rows, at(0, pair)] = jnp.where(
                    head_lanes, outs[unit - 1], outs[unit]
                ).astype(jnp.bfloat16)
                log_totals[pair, rows, :] = jnp.where(head_lanes, logs[unit], logs[unit - 1])

        units = 2 * pairs
        score(0)
        for unit in range(units):
            if unit + 1 < units:
                score(unit + 1)
            soften(unit)
            if unit > 0:
                gather(unit - 1)
        gather(units - 1)

    for block in range(blocks):
        attend(block)
        if block == 0:
            for copy in loads[4:]:
                copy.wait()
            pl.semaphore_wait(barrier, len(strides) + 1)
        send_part(0, block, dot(context[rows_of(block), :], output_weight[...], 1, 0))

    def normalized(values):
        centered = values - jnp.mean(values, axis=-1, keepdims=True)
        variance = jnp.mean(centered * centered, axis=-1, keepdims=True)
        inverse = lax.rsqrt(variance + EPSILON)
        return centered * inverse, inverse

    def pull_norm(grad, hat, inverse):
        return inverse * (
            grad
            - jnp.mean(grad, axis=-1, keepdims=True)
            - hat * jnp.mean(grad * hat, axis=-1, keepdims=True)
        )

    def first_norm(block):
        rows = rows_of(block)
        hat, inverse = normalized(
            tokens[rows, :].astype(jnp.float32) + both_parts(0, rows) + output_bias[...]
        )
        first_hat[rows, :] = hat
        row_facts[rows, 1:2] = inverse
        first_low[rows, :] = (hat * first_gain[...] + first_shift[...]).astype(jnp.bfloat16)

    tile = hidden // 4
    tiles = [slice(start, start + tile) for start in range(0, hidden, tile)]

    def hidden_units(block):
        rows = rows_of(block)
        for some in tiles:
            pre = dot(first_low[rows, :], up_weight[:, some], 1, 0) + up_bias[:, some]
            below = 0.5 + 0.5 * lax.erf(pre * math.sqrt(0.5))
            density = jnp.exp(-0.5 * pre * pre) * (1.0 / math.sqrt(2.0 * math.pi))
            inner[rows, some] = (pre * below).astype(jnp.bfloat16)
            slope[rows, some] = (below + pre * density).astype(jnp.bfloat16)

    def second_norm(block):
        rows = rows_of(block)
        first = first_hat[rows, :] * first_gain[...] + first_shift[...]
        hat, inverse = normalized(first + both_parts(1, rows) + down_bias[...])
        grad = cotangent[rows, :].astype(jnp.float32) * row_facts[rows, 0:1]
        cotangent[rows, :] = (hat * second_gain[...] + second_shift[...]).astype(jnp.bfloat16)
        back = pull_norm(grad * second_gain[...], hat, inverse)
        d_resid[rows, :] = back
        grad_low[rows, :] = back.astype(jnp.bfloat16)
        add_vector(4, grad * hat)
        add_vector(5, grad)
        add_vector(3, back)

    def through_hidden(block):
        rows = rows_of(block)
        for some in tiles:
            grad = dot(grad_low[rows, :], down_weight[some, :], 1, 1)
            low = (grad * slope[rows, some].astype(jnp.float32)).astype(jnp.bfloat16)
            d_pre[rows, some] = low
            up_bias_sums[:, some] = up_bias_sums[:, some] + column_sums(low.astype(jnp.float32))
        send_part(2, block, dot(d_pre[rows, :], up_weight[...], 1, 1))

    part_copy(0, 0).wait_recv()
    first_norm(0)
    for block in range(blocks):
        if block + 1 < blocks:
            part_copy(0, block + 1).wait_recv()
        if block >= 2:
            part_copy(1, block - 2).wait_recv()
        hidden_units(block)
        if block + 1 < blocks:
            first_norm(block + 1)
        if block >= 2:
            second_norm(block - 2)
        send_part(1, block, dot(inner[rows_of(block), :], down_weight[...], 1, 0))
    late = max(0, blocks - 2)
    for block in range(late, blocks):
        part_copy(1, block).wait_recv()
        second_norm(block)
        if block == late:
            through_hidden(0)
    columns = lambda place: slice(place * shard, (place + 1) * shard)
    quarters = hidden // shard
    sources = [down_blocks.at[place] for place in range(quarters)]
    sources += [up_blocks.at[place] for place in range(quarters)]
    sources += [inner.at[:width, columns(place)] for place in range(4)]

    chains = [
        Reduction(
            sources[c],
            totals.at[c],
            block_landings.at[c],
            chain_send.at[c],
            chain_recv.at[c],
            plans[c],
            dp,
            mp,
        )
        for c in range(count)
    ]
    chains.append(
        Reduction(
            vectors,
            vector_total,
            vector_landing,
            vector_send,
            vector_recv,
            vector_plan,
            dp,
            mp,
        )
    )
    point = iter(SCHEDULE)

    def move_chains():
        for c in next(point, ()):
            chains[c].advance()

    down_places = [(top, left) for top in range(0, hidden, width) for left in range(0, width, shard)]
    for place, (top, left) in enumerate(down_places):
        down_blocks[place] = dot(
            inner[:, top : top + width], grad_low[:, left : left + shard], 0, 0
        ).astype(jnp.bfloat16)
        move_chains()

    for block in range(1, blocks):
        through_hidden(block)
        move_chains()

    def first_norm_back(block):
        rows = rows_of(block)
        grad = d_resid[rows, :] + both_parts(2, rows)
        hat = first_hat[rows, :]
        back = pull_norm(grad * first_gain[...], hat, row_facts[rows, 1:2])
        d_resid[rows, :] = back
        grad_low[rows, :] = back.astype(jnp.bfloat16)
        add_vector(1, grad * hat)
        add_vector(2, grad)
        add_vector(0, back)

    for turn in range(max(quarters, blocks)):
        if turn < blocks:
            part_copy(2, turn).wait_recv()
        if turn < quarters:
            up_blocks[turn] = dot(first_low[...], d_pre[:, columns(turn)], 0, 0).astype(
                jnp.bfloat16
            )
        if turn < blocks:
            first_norm_back(turn)
        move_chains()
    for block in range(blocks):
        rows = rows_of(block)
        d_pre[rows, :shard] = dot(grad_low[rows, :], output_weight[...], 1, 1).astype(jnp.bfloat16)

    for start in range(0, width, shard):
        inner[start : start + shard, columns(0)] = dot(
            context[...], grad_low[:, start : start + shard], 0, 0
        ).astype(jnp.bfloat16)
    move_chains()

    first_hat[...] = jnp.zeros_like(first_hat)

    cross = (
        (lax.broadcasted_iota(jnp.int32, (PAIR, 1), 0) < HEAD_DIM) != head_lanes
    ).astype(jnp.float32)
    cross = cross.astype(jnp.bfloat16)

    def attend_back(block):
        low, high = key_window(block, row_count)
        rows = slice(block * BLOCK, (block + 1) * BLOCK)
        prepared, scored, weighed, d_queries = {}, {}, {}, {}

        def prepare(pair):
            query, grad = qkv[rows, at(0, pair)], d_pre[rows, at(0, pair)]
            product = grad.astype(jnp.float32) * context[rows, at(0, pair)].astype(jnp.float32)
            most = product.astype(jnp.bfloat16)
            rest = (product - most.astype(jnp.float32)).astype(jnp.bfloat16)
            mean = dot(most, cross, 1, 0) + dot(rest, cross, 1, 0)
            log_total = log_totals[pair, rows, :]
            prepared[pair] = []
            for head in range(2):
                own_query, own_grad = query * keep_head[head], grad * keep_head[head]
                less_log = in_parts(head, -log_total, run_of[head, rows, :])
                less_mean = in_parts(head, -mean, jnp.zeros_like(mean))
                prepared[pair].append(
                    (own_query, own_grad, own_query + less_log, own_grad + less_mean)
                )

        def score(pair, start):
            if start == low:
                prepare(pair)
            keys = slice(start, start + BLOCK)
            got = []
            for head in range(2):
                key = qkv[keys, at(1, pair)] * keep_head[head] + not_run_of[head, keys, :]
                value = qkv[keys, at(2, pair)] * keep_head[head] + ones_lanes[head].astype(
                    jnp.bfloat16
                )
                got.append(
                    (
                        dot(key, prepared[pair][head][2], 1, 1),
                        dot(value, prepared[pair][head][3], 1, 1),
                    )
                )
            scored[pair, start] = got

        def weigh(pair, start):
            got = []
            for scores, d_weights in scored.pop((pair, start)):
                weights = jnp.exp(scores)
                got.append(
                    (weights.astype(jnp.bfloat16), (weights * d_weights).astype(jnp.bfloat16))
                )
            weighed[pair, start] = got

        def gather(pair, start):
            keys = slice(start, start + BLOCK)
            key = qkv[keys, at(1, pair)]
            d_key = d_value = 0.0
            for head, (weights, d_scores) in enumerate(weighed.pop((pair, start))):
                d_value = d_value + dot(weights, prepared[pair][head][1], 1, 0)
                d_key = d_key + dot(d_scores, prepared[pair][head][0], 1, 0)
                d_query = dot(d_scores, key, 0, 0)
                d_queries[pair, head] = d_queries.get((pair, head), 0.0) + d_query
            first_hat[keys, at(0, pair)] = first_hat[keys, at(0, pair)] + d_key
            first_hat[keys, at(1, pair)] = first_hat[keys, at(1, pair)] + d_value
            if start + BLOCK == high:
                both = jnp.where(head_lanes, d_queries[pair, 0], d_queries[pair, 1])
                slope[rows, at(0, pair)] = (both * scale).astype(jnp.bfloat16)

        units = [(pair, start) for pair in range(pairs) for start in range(low, high, BLOCK)]
        score(*units[0])
        for place, unit in enumerate(units):
            if place + 1 < len(units):
                score(*units[place + 1])
            weigh(*unit)
            if place > 0:
                gather(*units[place - 1])
            if unit[1] + BLOCK == high:
                move_chains()
        gather(*units[-1])

    for block in range(blocks):
        attend_back(block)

    def round_keys(strip):
        rows = pl.ds(pl.multiple_of(strip * STRIP, STRIP), STRIP)
        slope[rows, shard : 3 * shard] = first_hat[rows, :].astype(jnp.bfloat16)

    each(row_count // STRIP, round_keys, 4)

    move_chains()

    for place in range(3):
        inner[:width, columns(1 + place)] = dot(tokens[...], slope[:, columns(place)], 0, 0).astype(
            jnp.bfloat16
        )
        move_chains()

    def finish_vectors():
        for place in range(6):
            vectors[place : place + 1, :] = jnp.sum(vector_sums[place], axis=0, keepdims=True)
        up_sum = jnp.sum(up_bias_sums[...], axis=0, keepdims=True)
        for place in range(hidden // width):
            vectors[6 + place : 7 + place, :] = up_sum[:, place * width : (place + 1) * width]
        ones = jnp.ones((16, row_count), jnp.bfloat16)
        last = 6 + hidden // width
        vectors[last : last + 1, :shard] = dot(ones, slope[:, :shard], 1, 0)[:1]
        vectors[last : last + 1, shard:] = dot(ones, slope[:, 2 * shard : 3 * shard], 1, 0)[:1]

    finish_vectors()
    move_chains()

    def token_part(block):
        rows = rows_of(block)
        send_part(3, block, dot(slope[rows, : 3 * shard], qkv_weight[...], 1, 1))

    for block in range(blocks):
        token_part(block)
        move_chains()

    def tokens_back(block):
        part_copy(3, block).wait_recv()

        rows = rows_of(block)
        tokens[rows, :] = (d_resid[rows, :] + both_parts(3, rows)).astype(jnp.bfloat16)

    for block in range(blocks):
        tokens_back(block)
        move_chains()

    move_chains()
    while any(chain.next_step <= len(chain.steps) for chain in chains):
        for chain in chains:
            chain.advance()

    for turn in (2, 3):
        for block in range(blocks):
            part_copy(turn, block).wait_send()


def widen_kernel(shard, result, tokens_grad, sums, vectors, *refs):
    (
        result_out,
        tokens_out,
        query_out,
        query_bias_out,
        key_out,
        value_out,
        value_bias_out,
        output_out,
        output_bias_out,
        first_gain_out,
        first_shift_out,
        up_out,
        up_bias_out,
        down_out,
        down_bias_out,
        second_gain_out,
        second_shift_out,
        wide,
        pass_sem,
        store_sem,
    ) = refs
    count, width = sums.shape[0], sums.shape[1]
    hidden = up_out.shape[1]
    passes = [
        pltpu.make_async_copy(source, target, pass_sem.at[i])
        for i, (source, target) in enumerate([(result, result_out), (tokens_grad, tokens_out)])
    ]
    for copy in passes:
        copy.start()
    for row, out in [
        (0, output_bias_out),
        (1, first_gain_out),
        (2, first_shift_out),
        (3, down_bias_out),
        (4, second_gain_out),
        (5, second_shift_out),
    ]:
        out[...] = vectors[row]
    for place in range(hidden // width):
        up_bias_out[place * width : (place + 1) * width] = vectors[6 + place]
    last = 6 + hidden // width
    query_bias_out[...] = vectors[last, :shard]
    value_bias_out[...] = vectors[last, shard:]

    targets = [
        down_out.at[top : top + width, left : left + shard]
        for top in range(0, hidden, width)
        for left in range(0, width, shard)
    ]
    targets += [up_out.at[:, left : left + shard] for left in range(0, hidden, shard)]
    targets += [None, query_out, key_out, value_out]
    stores = []
    for c in range(count):
        wide[c] = sums[c].astype(jnp.float32)
        if targets[c] is None:
            pieces = [
                (wide.at[c, left : left + shard], output_out.at[:, left : left + shard])
                for left in range(0, width, shard)
            ]
        else:
            pieces = [(wide.at[c], targets[c])]
        for piece, (source, target) in enumerate(pieces):
            stores.append(pltpu.make_async_copy(source, target, store_sem.at[c, piece]))
            stores[-1].start()
    for copy in stores + passes:
        copy.wait()


SCHEDULE = [
    (0,),
    (1,),
    (2,),
    (3,),
    (),
    (),
    (),
    (),
    (),
    (0, 1, 2, 4, 5),
    (3,),
    (),
    (2, 0, 6),
    (1,),
    (0, 7),
    (1, 2),
    (3, 4),
    (0, 1),
    (5, 8),
    (2, 0),
    (6, 3, 2),
    (1,),
    (3, 7, 5, 0),
    (4,),
    (5,),
    (3, 6, 9),
    (4,),
    (1, 0, 5, 11),
    (4, 6, 12),
    (),
    (),
    (),
    (5,),
    (4, 10),
    (),
    (),
    (6, 1, 7, 12, 3, 5, 6, 4, 0, 7, 2, 8, 12, 11, 6, 4, 10, 1, 7, 9, 7, 12, 8, 2, 3, 11, 5, 8, 10, 7, 12, 11, 4, 8, 11, 10, 9, 11, 6, 2, 8, 10, 3, 7, 11, 5, 9, 10, 8, 9, 10, 9, 11, 7, 8, 6, 9, 10, 9, 11, 8, 10, 9),
]


def local(
    tokens,
    cotangent,
    lengths,
    query_weight,
    query_bias,
    key_weight,
    value_weight,
    value_bias,
    output_weight,
    output_bias,
    first_gain,
    first_shift,
    up_weight,
    up_bias,
    down_weight,
    down_bias,
    second_gain,
    second_shift,
):
    row_count, width = tokens.shape
    shard, hidden = query_weight.shape[1], up_weight.shape[1]
    dp_size = lax.axis_size("dp")
    blocks = row_count // BLOCK
    low, wide = jnp.bfloat16, jnp.float32
    count = 2 * (hidden // shard) + 4
    orders = exchange_orders(dp_size)
    plans = [plan_steps(width, orders[i % len(orders)]) for i in range(count)]
    vector_rows = ROW_TILE
    vector_plan = [(stride, vector_rows, "whole") for stride in orders[0]]
    landing = max(landing_rows(plan) for plan in plans)
    steps = max(len(plan) for plan in plans)
    hbm = pl.BlockSpec(memory_space=pl.ANY)
    vmem = pl.BlockSpec(memory_space=pltpu.VMEM)
    smem = pl.BlockSpec(memory_space=pltpu.SMEM)
    dma = pltpu.SemaphoreType.DMA
    anywhere = lambda shape, dtype: (jax.ShapeDtypeStruct(shape, dtype), hbm)
    outs = pl.pallas_call(
        functools.partial(layer_kernel, plans, vector_plan, bits_of(dp_size)),
        out_shape=[
            pltpu.VMEM((row_count, width), low),
            pltpu.VMEM((row_count, width), low),
            pltpu.VMEM((count, width, shard), low),
            pltpu.VMEM((vector_rows, width), wide),
        ],
        in_specs=[hbm, hbm, smem] + [hbm] * 6 + [vmem] * 9,
        out_specs=[vmem] * 4,
        scratch_shapes=[
            pltpu.VMEM((width, 3 * shard), low),
            pltpu.VMEM((shard, width), low),
            pltpu.VMEM((width, hidden), low),
            pltpu.VMEM((hidden, width), low),
            pltpu.VMEM((row_count, 3 * shard), low),
            pltpu.VMEM((row_count, shard), low),
            pltpu.VMEM((shard // PAIR, row_count, PAIR), wide),
            pltpu.VMEM((row_count, 2), wide),
            pltpu.VMEM((2, row_count, PAIR), low),
            pltpu.VMEM((2, row_count, PAIR), low),
            pltpu.VMEM((2, row_count, width), low),
            pltpu.VMEM((2, row_count, width), low),
            pltpu.VMEM((row_count, width), wide),
            pltpu.VMEM((row_count, width), low),
            pltpu.VMEM((row_count, hidden), low),
            pltpu.VMEM((row_count, hidden), low),
            pltpu.VMEM((row_count, hidden), low),
            pltpu.VMEM((row_count, width), wide),
            pltpu.VMEM((row_count, width), low),
            pltpu.VMEM((hidden // shard, width, shard), low),
            pltpu.VMEM((hidden // shard, width, shard), low),
            pltpu.VMEM((6, 8, width), wide),
            pltpu.VMEM((8, hidden), wide),
            pltpu.VMEM((vector_rows, width), wide),
            pltpu.VMEM((count, landing, shard), low),
            pltpu.VMEM((max(1, len(vector_plan)) * vector_rows, width), wide),
            pltpu.VMEM((16, hidden), wide),
            dma((8,)),
            dma((4, blocks)),
            dma((4, blocks)),
            dma((count, steps)),
            dma((count, steps)),
            dma((max(1, len(vector_plan)),)),
            dma((max(1, len(vector_plan)),)),
        ],
        compiler_params=pltpu.CompilerParams(
            collective_id=0, has_side_effects=True, vmem_limit_bytes=54 * 2**20
        ),
        name="layer",
    )(
        tokens,
        cotangent,
        lengths,
        query_weight,
        key_weight,
        value_weight,
        output_weight,
        up_weight,
        down_weight,
        query_bias,
        value_bias,
        output_bias,
        first_gain,
        first_shift,
        up_bias,
        down_bias,
        second_gain,
        second_shift,
    )
    vector = lambda size: (jax.ShapeDtypeStruct((size,), wide), vmem)
    square = anywhere((width, shard), wide)
    shapes, specs = zip(
        anywhere((row_count, width), low),
        anywhere((row_count, width), low),
        square,
        vector(shard),
        square,
        square,
        vector(shard),
        anywhere((shard, width), wide),
        vector(width),
        vector(width),
        vector(width),
        anywhere((width, hidden), wide),
        vector(hidden),
        anywhere((hidden, width), wide),
        vector(width),
        vector(width),
        vector(width),
    )
    return pl.pallas_call(
        functools.partial(widen_kernel, shard),
        out_shape=shapes,
        in_specs=[vmem] * 4,
        out_specs=specs,
        scratch_shapes=[
            pltpu.VMEM((count, width, shard), wide),
            dma((2,)),
            dma((count, width // shard)),
        ],
        compiler_params=pltpu.CompilerParams(vmem_limit_bytes=20 * 2**20),
        name="widen",
    )(*outs)


def solution(mesh):
    in_specs = (
        P("dp", None),
        P("dp", None),
        P("dp", None),
        P(None, "mp"),
        P("mp"),
        P(None, "mp"),
        P(None, "mp"),
        P("mp"),
        P("mp", None),
        P(),
        P(),
        P(),
        P(None, "mp"),
        P("mp"),
        P("mp", None),
        P(),
        P(),
        P(),
    )
    out_specs = (
        P("dp", None),
        P("dp", None),
        P(None, "mp"),
        P("mp"),
        P(None, "mp"),
        P(None, "mp"),
        P("mp"),
        P("mp", None),
        P(),
        P(),
        P(),
        P(None, "mp"),
        P("mp"),
        P("mp", None),
        P(),
        P(),
        P(),
    )
    return jax.shard_map(local, mesh=mesh, in_specs=in_specs, out_specs=out_specs, check_vma=False)
```
